512 devices in a mesh: shard: 128 (over x, z, core), head: 4 (over y).
Axes of the slice: x: 4, y: 4, z: 16, core: 2. Of those that a mesh axis runs over, the one named last changes fastest.
Arguments:
- features: bfloat16 [32768, 1024], P('shard'), may hold values from -6 to 6
- owners: int32 [32768, 1], P('shard'), may hold values from 0 to 127; in each aligned block of 256 rows (0 to 255, 256 to 511, ...) at most 3 rows name the same one
- query_local: int32 [32768], P('shard'), may hold values from 0 to 15
- grades: int32 [32768], P('shard'), may hold values from 0 to 4
- query_weight: float32 [2048], P('shard'), may hold values from 0.3 to 36
- norm_gain: float32 [1024], replicated, may hold values from 0.25 to 1.75
- qkv_weight: bfloat16 [1024, 3, 1024], P(None, None, 'head'), may hold values from -1 to 1
- out_weight: bfloat16 [1024, 1024], P('head'), may hold values from -0.1875 to 0.1875
- score_weight: float32 [1024], P('head'), may hold values from -0.1875 to 0.1875
Outputs:
- encoded: bfloat16 [32768, 1024], P('shard', 'head')
- score_vals: float32 [32768], P('shard')
- score_grads: float32 [32768], P('shard')
- loss: float32 [], replicated
The draws below stay inside these ranges and needn't reach their ends.
Inputs may be any that keep to these rules, and one draw needn't show every extreme that they name: `owners`: in the rows of one crawl shard no owner is named more than 3 times, a bound that some block reaches.
All inputs are finite; a program needn't handle non-finite values.
Results may differ from the reference program's by a relative error of at most 0.03.
Values may be sent and summed in bfloat16 or wider, within the bound.
A program may use at most 64 MiB of HBM per device.

```python
import math
import jax
import jax.numpy as jnp
import numpy as np
from jax import lax

D = 1024
HEADS = 16
HEAD_DIM = 64
DOC_DEV = 256
QRY_DEV = 16
SLOTS = 384
CAP = 3
DOCS = 32768
QUERIES = 2048
N_SHARD = 128
N_HEAD = 4


def common_direction(key):
    return jax.random.uniform(jax.random.fold_in(key, 91), (D,), jnp.float32, -1.0, 1.0)


def draw_features(key, part):
    direction = common_direction(key)
    key = jax.random.fold_in(key, 5)
    key_strength, key_noise = jax.random.split(key, 2)
    strength = jax.random.uniform(key_strength, (DOCS, 1), jnp.float32, 0.0, 3.9)
    noise = jax.random.truncated_normal(key_noise, -2.0, 2.0, (DOCS, D), jnp.float32)
    return (strength * direction[None, :] + noise).astype(jnp.bfloat16)


def draw_qkv_weight(key, part):
    direction = common_direction(key)
    key = jax.random.fold_in(key, 7)
    key_base, key_strength = jax.random.split(key, 2)
    base = jax.random.truncated_normal(key_base, -4.0, 4.0, (D, 3, D), jnp.float32)
    head_strength = jax.random.uniform(key_strength, (HEADS,), jnp.float32, 0.85, 1.0) * math.sqrt(1000.0 / math.sqrt(HEAD_DIM))
    column_strength = jnp.repeat(head_strength, HEAD_DIM)
    aligned = direction[:, None] * column_strength[None, :] / D
    extra = jnp.stack([aligned, aligned, jnp.zeros_like(aligned)], axis=1)
    return (base / math.sqrt(D) + extra).astype(jnp.bfloat16)


def rising_weights(key, rise):
    position = (jnp.arange(QUERIES, dtype=jnp.int32) // QRY_DEV).astype(jnp.float32) / max(N_SHARD - 1, 1)
    jitter = jnp.exp(jax.random.uniform(key, (QUERIES,), jnp.float32, 0.0, math.log(4.0)))
    return 0.3 * jnp.exp(position * math.log(rise)) * jitter


def draw_query_weight(key, part):
    key = jax.random.fold_in(key, 11)
    values = rising_weights(key, 10.0)
    return values.astype(jnp.float32)


def place_ends(entries, rng, least, high):
    index_at = [jax.random.randint(jax.random.fold_in(rng, axis), (), 0, length) for axis, length in enumerate(entries.shape)]
    longest = entries.shape.index(max(entries.shape))
    neighbour = index_at[:longest] + [(index_at[longest] + 1) % entries.shape[longest]] + index_at[longest + 1:]
    return entries.at[tuple(index_at)].set(least).at[tuple(neighbour)].set(high)


def steps_of(stream_key, shape, cuts, least, high):
    factor_of = 1.0
    for dim, shards_of in cuts:
        draws = jax.random.uniform(jax.random.fold_in(jax.random.fold_in(stream_key, 6), dim), (shards_of,), jnp.float32, least / len(cuts), high / len(cuts))
        factor_of = factor_of * jnp.repeat(jnp.exp(draws), shape[dim] // shards_of).reshape((-1,) + (1,) * (len(shape) - 1 - dim))
    return factor_of


def routed_block(own_key, own, number, rows, count, top, bound, slope):
    ranking = jax.random.permutation(own_key, count)
    packed, common = portions_of(count, rows * top, bound, slope, True), portions_of(count, rows * top, bound, slope, False)
    places = jnp.arange(count)

    def named(tallies, offset_by):
        used = int((tallies > 0).sum())
        fixed = max(1, used // 4)
        shifted = fixed + (places - fixed + offset_by * (used - fixed)) % max(1, count - fixed)
        return jnp.zeros((count,), jnp.int32).at[ranking[jnp.where(places < fixed, places, shifted)]].set(jnp.asarray(tallies, jnp.int32))

    tallies = jnp.where(number % 4 == 0, named(packed, number // 4), named(common, number - number // 4 - 1))
    mixed = jax.random.permutation(jax.random.fold_in(own, 3), count)
    source_of, sink = mixed[0:count // 2 * 2:2], mixed[1:count // 2 * 2:2]
    room = jnp.minimum(tallies[source_of] - 1, bound - tallies[sink]) // 2
    room = jnp.where((source_of == ranking[0]) | (sink == ranking[0]) | (tallies[sink] == 0), 0, jnp.maximum(room, 0))
    shifted = jax.random.randint(jax.random.fold_in(own, 4), (count // 2,), 0, 1 << 20) % (room + 1)
    tallies = tallies.at[source_of].add(-shifted).at[sink].add(shifted)
    items = jnp.searchsorted(jnp.cumsum(tallies), jnp.arange(rows * top), side="right").astype(jnp.int32)
    listing = items.reshape(top, rows).T
    listing = listing[jax.random.permutation(jax.random.fold_in(own, 1), rows)]
    offset_by = jax.random.randint(jax.random.fold_in(own, 2), (rows, 1), 0, top)
    return jnp.take_along_axis(listing, (jnp.arange(top)[None, :] + offset_by) % top, axis=1)


def portions_of(count, total, most, lean, full):
    loads = [(1 << 20) // math.isqrt(grade ** lean) + 1 for grade in range(1, count + 1)]
    largest = most if full else min(most, max(-(-total // count), total * loads[0] // sum(loads)))
    least = 1 if total - largest >= count - 1 else 0
    counts, spare = [largest] + [least] * (count - 1), total - largest - least * (count - 1)
    while spare > 0:
        movable = [i for i in range(1, count) if counts[i] < largest] or [i for i in range(1, count) if counts[i] < most]
        mass, budget = sum([loads[i] for i in movable]), spare
        for i in movable:
            more = min(most - counts[i], max(1, budget * loads[i] // mass), spare)
            counts[i] = counts[i] + more
            spare = spare - more
    return np.array(counts)


def normal_values(own_key, shape, scale, most, shards=(), kind=jnp.bfloat16):
    entries = scale * jax.random.normal(own_key, shape, jnp.float32)
    if shards:
        entries = entries * steps_of(own_key, shape, shards, -0.22, 0.18)
    return jnp.clip(entries, -most, most).astype(kind)


def setup_inputs(seed: int = 0) -> dict:
    key_list = jax.random.split(jax.random.key(seed), 10)
    features = draw_features(jax.random.fold_in(key_list[9], 71), 0)
    owners_keys = jax.random.split(jax.random.fold_in(key_list[1], 1), DOCS // DOC_DEV)
    owners_turns = jax.random.permutation(jax.random.fold_in(key_list[1], 3), DOCS // DOC_DEV)
    owners = jax.vmap(lambda own, number: routed_block(jax.random.fold_in(key_list[1], 2), own, number, DOC_DEV, N_SHARD, 1, CAP, 2))(owners_keys, owners_turns).reshape((DOCS, 1))
    query_local = place_ends(jax.random.randint(key_list[2], (DOCS,), 0, QRY_DEV), jax.random.fold_in(key_list[2], 1), 0, QRY_DEV - 1).astype(jnp.int32)
    grades = place_ends(jax.random.randint(key_list[3], (DOCS,), 0, 5), jax.random.fold_in(key_list[3], 1), 0, 4).astype(jnp.int32)
    query_weight = draw_query_weight(jax.random.fold_in(key_list[9], 71), 0)
    norm_gain = jnp.clip(1.0 + 0.15 * jax.random.normal(key_list[5], (D,), jnp.float32), 0.25, 1.75)
    qkv_weight = draw_qkv_weight(jax.random.fold_in(key_list[9], 71), 0)
    out_weight = normal_values(key_list[7], (D, D), D ** -0.5, 0.1875, ((0, 4),))
    score_weight = normal_values(key_list[8], (D,), D ** -0.5, 0.1875, ((0, 4),), jnp.float32)
    return {"features": features, "owners": owners, "query_local": query_local, "grades": grades, "query_weight": query_weight, "norm_gain": norm_gain, "qkv_weight": qkv_weight, "out_weight": out_weight, "score_weight": score_weight}


eps_norm = 1e-06

def owner_slots(owners):
    owner_ids = owners[:, 0]
    source = jnp.arange(DOCS, dtype=jnp.int32) // DOC_DEV
    onehot = (owner_ids[:, None] == jnp.arange(N_SHARD, dtype=jnp.int32)[None, :]).astype(jnp.int32)
    blocks = onehot.reshape(N_SHARD, DOC_DEV, N_SHARD)
    before = (jnp.cumsum(blocks, axis=1) - blocks).reshape(DOCS, N_SHARD)
    bucket_rank = lax.optimization_barrier(jnp.sum(before * onehot, axis=1))
    return (owner_ids * SLOTS + source * CAP + bucket_rank).astype(jnp.int32)

def owner_block(rows, query_ids, grade_vals, weight_table, norm_gain, qkv_weight, out_weight, score_weight):
    rows_f = rows.astype(jnp.float32)
    normed = (rows_f * lax.rsqrt(lax.optimization_barrier(jnp.mean(rows_f * rows_f, axis=1, keepdims=True)) + eps_norm) * norm_gain).astype(jnp.bfloat16)
    queries = jnp.dot(normed, qkv_weight[:, 0, :], preferred_element_type=jnp.float32).astype(jnp.bfloat16).reshape(SLOTS, HEADS, HEAD_DIM)
    key_rows = jnp.dot(normed, qkv_weight[:, 1, :], preferred_element_type=jnp.float32).astype(jnp.bfloat16).reshape(SLOTS, HEADS, HEAD_DIM)
    value_rows = jnp.dot(normed, qkv_weight[:, 2, :], preferred_element_type=jnp.float32).astype(jnp.bfloat16).reshape(SLOTS, HEADS, HEAD_DIM)
    scores = jnp.einsum('shd,thd->hst', queries.astype(jnp.float32), key_rows.astype(jnp.float32)) / math.sqrt(HEAD_DIM)
    valid = query_ids >= 0
    same = (query_ids[:, None] == query_ids[None, :]) & valid[:, None] | jnp.eye(SLOTS, dtype=bool)
    scores = jnp.where(same[None], scores, -jnp.inf)
    peak = lax.optimization_barrier(jnp.max(scores, axis=2, keepdims=True))
    expo = jnp.exp(scores - peak)
    probs = (expo / lax.optimization_barrier(jnp.sum(expo, axis=2, keepdims=True))).astype(jnp.bfloat16)
    context = jnp.einsum('hst,thd->shd', probs.astype(jnp.float32), value_rows.astype(jnp.float32)).astype(jnp.bfloat16)
    groups = context.reshape(SLOTS, N_HEAD, D // N_HEAD).astype(jnp.float32)
    parts = jnp.einsum('sgf,gfd->gsd', groups, out_weight.reshape(N_HEAD, D // N_HEAD, D).astype(jnp.float32)).astype(jnp.bfloat16)
    mixed = rows_f + lax.optimization_barrier(jnp.sum(parts.astype(jnp.float32), axis=0))
    score_row = lax.optimization_barrier(jnp.sum(mixed * score_weight, axis=1)) * lax.rsqrt(lax.optimization_barrier(jnp.sum(mixed * mixed, axis=1)) / D + eps_norm)
    row_weight = lax.optimization_barrier(jnp.sum((query_ids[:, None] == jnp.arange(QRY_DEV, dtype=jnp.int32)[None, :]).astype(jnp.float32) * weight_table[None, :], axis=1))
    better = (same & valid[:, None] & valid[None, :] & (grade_vals[:, None] > grade_vals[None, :])).astype(jnp.float32)
    spread = score_row[None, :] - score_row[:, None]
    weighted = better * row_weight[:, None]
    pair_sum = jnp.sum(weighted * jax.nn.softplus(spread))
    pair_count = jnp.sum(better)
    pulled = weighted * jax.nn.sigmoid(spread)
    pull = lax.optimization_barrier(jnp.sum(pulled, axis=0)) - lax.optimization_barrier(jnp.sum(pulled, axis=1))
    return (mixed.astype(jnp.bfloat16), score_row, pair_sum, pair_count, pull)

def reference(features, owners, query_local, grades, query_weight, norm_gain, qkv_weight, out_weight, score_weight):
    flat = owner_slots(owners)
    table = jnp.zeros((N_SHARD * SLOTS, D), jnp.bfloat16).at[flat].set(features).reshape(N_SHARD, SLOTS, D)
    query_table = jnp.full((N_SHARD * SLOTS,), -1, jnp.int32).at[flat].set(query_local).reshape(N_SHARD, SLOTS)
    grade_table = jnp.zeros((N_SHARD * SLOTS,), jnp.int32).at[flat].set(grades).reshape(N_SHARD, SLOTS)
    weight_tables = query_weight.reshape(N_SHARD, QRY_DEV)

    def one_owner(items):
        return owner_block(items[0], items[1], items[2], items[3], norm_gain, qkv_weight, out_weight, score_weight)
    encoded, score_rows, pair_sums, pair_counts, pulls = lax.map(one_owner, (table, query_table, grade_table, weight_tables))
    pair_total = jnp.maximum(jnp.sum(pair_counts), jnp.float32(1.0))
    loss = jnp.sum(pair_sums) / pair_total
    grads = pulls.reshape(-1) / pair_total
    return (encoded.reshape(-1, D)[flat], score_rows.reshape(-1)[flat], grads[flat], loss)
```

```python
import math

import jax
import jax.numpy as jnp
from jax import lax
from jax.sharding import PartitionSpec as P

HEAD_DIM = 64


eps_norm = 1e-06


def block_rows(whole_rows):
    number_blocks = max(1, whole_rows // 512)
    while whole_rows % number_blocks != 0:
        number_blocks = number_blocks - 1
    return whole_rows // number_blocks


def body(
    features,
    owners,
    query_local,
    grades,
    query_weight,
    norm_gain,
    qkv_weight,
    out_weight,
    score_weight,
):
    shards = lax.axis_size("shard")
    head_count = lax.axis_size("head")
    doc_rows = features.shape[0]
    slot_rows = 3 * doc_rows // 2
    capacity = slot_rows // shards
    local_width = out_weight.shape[0]
    model_width = out_weight.shape[1]
    local_heads = local_width // HEAD_DIM
    head_index = lax.axis_index("head")
    query_count = query_weight.shape[0]
    owner_ids = owners[:, 0]
    onehot = (owner_ids[:, None] == jnp.arange(shards, dtype=jnp.int32)[None, :]).astype(jnp.int32)
    bucket_rank = jnp.sum((jnp.cumsum(onehot, axis=0) - onehot) * onehot, axis=1)
    slot_index = owner_ids * capacity + bucket_rank
    meta_rows = jnp.stack([query_local + 1, grades], axis=1).astype(jnp.bfloat16)
    own_cols = lax.dynamic_slice_in_dim(features, head_index * local_width, local_width, 1)
    send = jnp.zeros((slot_rows, local_width + 2), jnp.bfloat16).at[slot_index].set(
        jnp.concatenate([own_cols, meta_rows], axis=1)
    )
    recv = lax.all_to_all(send, "shard", split_axis=0, concat_axis=0, tiled=True)
    own_full = recv[:, :local_width]
    rows_full = lax.all_gather(own_full, "head", axis=1, tiled=True)
    query_ids = recv[:, local_width].astype(jnp.int32) - 1
    grade_vals = recv[:, local_width + 1].astype(jnp.int32)
    row_weight = jnp.sum(
        (query_ids[:, None] == jnp.arange(query_count, dtype=jnp.int32)[None, :]).astype(
            jnp.float32
        )
        * query_weight[None, :],
        axis=1,
    )
    rows_f = rows_full.astype(jnp.float32)
    normed = (
        rows_f * lax.rsqrt(jnp.mean(rows_f * rows_f, axis=1, keepdims=True) + eps_norm) * norm_gain
    ).astype(jnp.bfloat16)
    projected = jnp.dot(
        normed, qkv_weight.reshape(model_width, 3 * local_width), preferred_element_type=jnp.float32
    ).astype(jnp.bfloat16)
    projected = projected.reshape(slot_rows, 3, local_heads, HEAD_DIM)
    queries = projected[:, 0]
    key_rows = projected[:, 1]
    value_rows = projected[:, 2]
    rows_per = block_rows(slot_rows)
    block_count = slot_rows // rows_per
    slot_pos = jnp.arange(slot_rows, dtype=jnp.int32)
    valid = query_ids >= 0
    block_starts = jnp.arange(block_count, dtype=jnp.int32) * rows_per

    def block_mask(block_ids, start):
        block_pos = start + jnp.arange(rows_per, dtype=jnp.int32)
        return (block_ids[:, None] == query_ids[None, :]) & (block_ids >= 0)[:, None] | (
            block_pos[:, None] == slot_pos[None, :]
        )

    def attend(items):
        block_queries, block_ids, start = items
        scores = jnp.einsum(
            "shd,thd->hst", block_queries, key_rows, preferred_element_type=jnp.float32
        ) / math.sqrt(HEAD_DIM)
        same = block_mask(block_ids, start)
        scores = jnp.where(same[None], scores, -jnp.inf)
        peak = jnp.max(scores, axis=2, keepdims=True)
        expo = jnp.exp(scores - peak)
        probs = (expo / jnp.sum(expo, axis=2, keepdims=True)).astype(jnp.bfloat16)
        return jnp.einsum(
            "hst,thd->shd", probs, value_rows, preferred_element_type=jnp.float32
        ).astype(jnp.bfloat16)

    context = lax.map(
        attend,
        (
            queries.reshape(block_count, rows_per, local_heads, HEAD_DIM),
            query_ids.reshape(block_count, rows_per),
            block_starts,
        ),
    )
    context = context.reshape(slot_rows, local_width)
    partial_out = jnp.dot(context, out_weight, preferred_element_type=jnp.float32)
    attended = lax.psum_scatter(
        partial_out.astype(jnp.bfloat16), "head", scatter_dimension=1, tiled=True
    ).astype(jnp.float32)
    mixed = own_full.astype(jnp.float32) + attended
    encoded_slots = mixed.astype(jnp.bfloat16)
    square_sum, weighted_sum = lax.psum(
        (jnp.sum(mixed * mixed, axis=1), jnp.dot(mixed, score_weight)), "head"
    )
    score_row = weighted_sum * lax.rsqrt(square_sum / (local_width * head_count) + eps_norm)

    def pair_block(items):
        block_scores, block_grades, block_ids, block_weight, start = items
        same = block_mask(block_ids, start)
        better = (
            same
            & (block_ids >= 0)[:, None]
            & valid[None, :]
            & (block_grades[:, None] > grade_vals[None, :])
        ).astype(jnp.float32)
        weighted = better * block_weight[:, None]
        spread = score_row[None, :] - block_scores[:, None]
        pulled = weighted * jax.nn.sigmoid(spread)
        return (
            jnp.sum(weighted * jax.nn.softplus(spread)),
            jnp.sum(better),
            jnp.sum(pulled, axis=1),
            jnp.sum(pulled, axis=0),
        )

    block_sums, block_counts, row_pulls, column_pulls = lax.map(
        pair_block,
        (
            score_row.reshape(block_count, rows_per),
            grade_vals.reshape(block_count, rows_per),
            query_ids.reshape(block_count, rows_per),
            row_weight.reshape(block_count, rows_per),
            block_starts,
        ),
    )
    pair_sum = jnp.sum(block_sums)
    pair_count = jnp.sum(block_counts)
    pull = jnp.sum(column_pulls, axis=0) - row_pulls.reshape(slot_rows)
    sums = jnp.concatenate(
        [jnp.broadcast_to(v[None], (slot_rows, 1)) for v in (pair_sum, pair_count)], axis=1
    )
    words = jnp.concatenate([score_row[:, None], pull[:, None], sums], axis=1)
    high = lax.reduce_precision(words, 8, 7)
    middle = lax.reduce_precision(words - high, 8, 7)
    low = words - high - middle
    back = lax.all_to_all(
        jnp.concatenate(
            [encoded_slots]
            + [piece.astype(jnp.bfloat16) for piece in (high, middle, low)],
            axis=1,
        ),
        "shard",
        split_axis=0,
        concat_axis=0,
        tiled=True,
    )
    tail = back[:, local_width:].astype(jnp.float32)
    tail = tail[:, 0:4] + tail[:, 4:8] + tail[:, 8:12]
    totals = jnp.sum(tail.reshape(shards, capacity, 4)[:, 0, 2:4], axis=0)
    pair_total = jnp.maximum(totals[1], jnp.float32(1.0))
    loss = totals[0] / pair_total
    picked = back[slot_index]
    encoded = picked[:, :local_width]
    words_back = tail[slot_index]
    return (encoded, words_back[:, 0], words_back[:, 1] / pair_total, loss)


def solution(mesh):
    placed = (
        P("shard", None),
        P("shard", None),
        P("shard"),
        P("shard"),
        P("shard"),
        P(),
        P(None, None, "head"),
        P("head", None),
        P("head"),
    )
    return jax.shard_map(
        body,
        mesh=mesh,
        in_specs=placed,
        out_specs=(P("shard", "head"), P("shard"), P("shard"), P()),
        check_vma=False,
    )
```

```python
import functools

import jax
import jax.numpy as jnp
from jax import lax
from jax.experimental import pallas as pl
from jax.experimental.pallas import tpu as pltpu
from jax.sharding import PartitionSpec as P

MESH = pl.DeviceIdType.MESH
HEAD_DIM = 64
CAP = 3
ROWS = 8
LANES = 128
eps_norm = 1e-06
F32 = jnp.float32
BF16 = jnp.bfloat16
NT = (((1,), (1,)), ((), ()))
TN = (((0,), (0,)), ((), ()))


def dot(a, b):
    return jnp.dot(a, b, preferred_element_type=F32)


def iota(shape, dim):
    return lax.broadcasted_iota(jnp.int32, shape, dim)


def layer_kernel(
    shards,
    heads,
    feat_ref,
    doc_ref,
    qw_ref,
    gain_ref,
    wqkv_hbm,
    wout_hbm,
    sw_ref,
    enc_ref,
    small_ref,
    wqkv,
    wout,
    send,
    recv,
    wide,
    gathered,
    proj,
    parts,
    landed,
    stats,
    back_send,
    back,
    local_sem,
    send_sem,
    recv_sem,
    y_send,
    y_recv,
):
    me = lax.axis_index("shard")
    head = lax.axis_index("head")
    docs = feat_ref.shape[0]
    width = wout_hbm.shape[0]
    model = wout_hbm.shape[1]
    slots = CAP * shards

    def peer(i):
        return lax.rem(me + i, shards)

    def head_peer(i):
        return lax.rem(head + i, heads)

    barrier = pltpu.get_barrier_semaphore()

    def greet(i, carry):
        pl.semaphore_signal(
            barrier, 1, device_id={"shard": peer(i)}, device_id_type=MESH
        )
        return carry

    lax.fori_loop(1, shards, greet, 0)
    for i in range(1, heads):
        pl.semaphore_signal(
            barrier, 1, device_id={"head": head_peer(i)}, device_id_type=MESH
        )
    load_qkv = pltpu.make_async_copy(wqkv_hbm, wqkv, local_sem.at[0])
    load_out = pltpu.make_async_copy(wout_hbm, wout, local_sem.at[1])
    load_qkv.start()
    load_out.start()

    owner = jnp.bitwise_and(doc_ref[0:1, :] - me, shards - 1)
    query = doc_ref[1:2, :].astype(F32) + 1.0
    grade = doc_ref[2:3, :].astype(F32)
    named = iota((shards, docs), 0) == owner
    named_f = named.astype(F32)
    earlier = (iota((docs, docs), 0) < iota((docs, docs), 1)).astype(F32).astype(BF16)
    before = dot(named_f.astype(BF16), earlier)
    rank_f = jnp.sum(before * named_f, axis=0, keepdims=True)
    rank = rank_f.astype(jnp.int32)
    first = owner * ROWS + 2 * rank
    block_row = iota((shards * ROWS, docs), 0)
    place = [
        (block_row == where).astype(F32).astype(BF16)
        for where in (first, first + 1, owner * ROWS + 2 * CAP)
    ]
    lane = iota((LANES, docs), 0)
    facts = jnp.where(lane == rank, query, 0.0) + jnp.where(
        lane == rank + CAP, grade, 0.0
    )
    left = pl.ds(pl.multiple_of(head * width, LANES), LANES)
    right = pl.ds(pl.multiple_of(head * width + LANES, LANES), LANES)
    block = dot(place[0], feat_ref[:, left]) + dot(place[1], feat_ref[:, right])
    block = block + lax.dot_general(
        place[2], facts.astype(BF16), NT, preferred_element_type=F32
    )
    send[...] = block.reshape(shards, ROWS, LANES).astype(BF16)

    pl.semaphore_wait(barrier, shards - 1 + heads - 1)

    def push(i, carry):
        pltpu.make_async_remote_copy(
            send.at[i],
            recv.at[i],
            send_sem.at[0],
            recv_sem.at[0],
            device_id={"shard": peer(i)},
            device_id_type=MESH,
        ).start()
        return carry

    lax.fori_loop(1, shards, push, 0)
    recv[0] = send[0]
    others = recv.at[pl.ds(1, shards - 1)]
    pltpu.make_async_copy(others, others, recv_sem.at[0]).wait()

    wide[...] = recv[...].astype(F32).reshape(shards * ROWS, LANES)

    def rows_of(j):
        return wide[pl.ds(j, shards, stride=ROWS), :]

    own = gathered.at[head]
    for r in range(CAP):
        for half in range(2):
            own[r * shards : (r + 1) * shards, half * LANES : (half + 1) * LANES] = (
                rows_of(2 * r + half).astype(BF16)
            )
    fact_cols = rows_of(2 * CAP)
    fact_rows = fact_cols.T

    def exchange(source, target, lane_of):
        copies = []
        for i in (2, 1, 3):
            copy = pltpu.make_async_remote_copy(
                source(head_peer(i)),
                target,
                y_send.at[lane_of, i],
                y_recv.at[lane_of, i],
                device_id={"head": head_peer(i)},
                device_id_type=MESH,
            )
            copy.start()
            copies.append(copy)
        return copies

    copies = exchange(lambda t: own, own, 0)
    query_col = jnp.concatenate([fact_cols[:, r : r + 1] for r in range(CAP)], axis=0)
    query_row = jnp.concatenate([fact_rows[r : r + 1, :] for r in range(CAP)], axis=1)
    grade_col = jnp.concatenate(
        [fact_cols[:, CAP + r : CAP + r + 1] for r in range(CAP)], axis=0
    )
    grade_row = jnp.concatenate(
        [fact_rows[CAP + r : CAP + r + 1, :] for r in range(CAP)], axis=1
    )
    diagonal = iota((slots, slots), 0) == iota((slots, slots), 1)
    related = (query_col == query_row) & (query_col > 0.5)
    bias = jnp.where(related | diagonal, 0.0, -jnp.inf)
    load_qkv.wait()
    load_out.wait()
    for copy in copies:
        copy.wait()

    squares = jnp.zeros((slots, 1), F32)
    total = jnp.zeros((slots, 3 * width), F32)
    for g in range(heads):
        x = gathered[g].astype(F32)
        squares = squares + jnp.sum(x * x, axis=1, keepdims=True)
        scaled = (x * gain_ref[:, g * width : (g + 1) * width]).astype(BF16)
        total = total + dot(scaled, wqkv[g * width : (g + 1) * width, :])
    proj[...] = (total * lax.rsqrt(squares / model + eps_norm)).astype(BF16)

    lane_col = iota((1, LANES), 1)
    context = []
    for pair in range(width // LANES):
        at = pair * LANES
        q2 = proj[:, at : at + LANES]
        k2 = proj[:, width + at : width + at + LANES]
        v2 = proj[:, 2 * width + at : 2 * width + at + LANES]
        mixed_heads = None
        for sub in range(LANES // HEAD_DIM):
            mine = (lane_col // HEAD_DIM) == sub
            q1 = jnp.where(mine, q2, jnp.zeros_like(q2))
            scores = (
                lax.dot_general(q1, k2, NT, preferred_element_type=F32)
                * (HEAD_DIM**-0.5)
                + bias
            )
            expo = jnp.exp(scores - jnp.max(scores, axis=1, keepdims=True))
            probs = (expo / jnp.sum(expo, axis=1, keepdims=True)).astype(BF16)
            out = dot(probs, v2)
            mixed_heads = out if sub == 0 else jnp.where(mine, out, mixed_heads)
        context.append(mixed_heads.astype(BF16))
    context = jnp.concatenate(context, axis=1)
    for g in range(heads):
        parts[g] = dot(context, wout[:, g * width : (g + 1) * width]).astype(BF16)
    copies = exchange(lambda t: parts.at[t], landed.at[head], 1)
    landed[head] = parts[head]
    for copy in copies:
        copy.wait()

    mixed = own[...].astype(F32)
    attended = landed[0].astype(F32)
    for g in range(1, heads):
        attended = attended + landed[g].astype(F32)
    mixed = mixed + attended
    encoded = mixed.astype(BF16).astype(F32)
    exact = lax.Precision.HIGHEST
    ones = jnp.ones((ROWS, width), F32)
    dotted = lax.dot_general(
        jnp.broadcast_to(sw_ref[...], (ROWS, width)),
        mixed,
        NT,
        precision=exact,
        preferred_element_type=F32,
    )
    squared = lax.dot_general(
        ones, mixed * mixed, NT, precision=exact, preferred_element_type=F32
    )
    stats[head] = jnp.where(iota((ROWS, slots), 0) == 0, dotted, squared)
    copies = exchange(lambda t: stats.at[head], stats.at[head], 2)
    for r in range(CAP):
        for half in range(2):
            wide[pl.ds(2 * r + half, shards, stride=ROWS), :] = encoded[
                r * shards : (r + 1) * shards, half * LANES : (half + 1) * LANES
            ]
    weight_row = jnp.zeros((1, slots), F32)
    for k in range(qw_ref.shape[1]):
        weight_row = weight_row + jnp.where(
            query_row == float(k + 1), qw_ref[0:1, k : k + 1], 0.0
        )
    for copy in copies:
        copy.wait()
    summed = stats[0]
    for g in range(1, heads):
        summed = summed + stats[g]
    score_row = summed[0:1, :] * lax.rsqrt(summed[1:2, :] / model + eps_norm)
    score_col = jnp.sum(jnp.where(diagonal, score_row, 0.0), axis=1, keepdims=True)

    above = grade_col - grade_row
    counted = jnp.where(
        related & (above != 0.0), jnp.where(above > 0.0, 1.0, -1.0), 0.0
    )
    spread = counted * (score_row - score_col)
    small = jnp.exp(-jnp.abs(spread))
    softplus = jnp.maximum(spread, 0.0) + jnp.log1p(small)
    sigmoid = jnp.where(spread >= 0.0, 1.0, small) / (1.0 + small)
    pull_row = weight_row * jnp.sum(counted * sigmoid, axis=0, keepdims=True)
    both = jnp.abs(counted)
    pair_row = weight_row * jnp.sum(both * softplus, axis=0, keepdims=True)
    pair_sum = 0.5 * jnp.sum(pair_row, axis=1, keepdims=True)
    pair_count = 0.5 * jnp.sum(
        jnp.sum(both, axis=0, keepdims=True), axis=1, keepdims=True
    )

    words = [score_row[:, r * shards : (r + 1) * shards] for r in range(CAP)]
    words += [pull_row[:, r * shards : (r + 1) * shards] for r in range(CAP)]
    words += [jnp.broadcast_to(v, (1, shards)) for v in (pair_sum, pair_count)]
    words = jnp.concatenate(words, axis=0)
    high = words.astype(BF16).astype(F32)
    middle = (words - high).astype(BF16).astype(F32)
    low = words - high - middle
    pieces = jnp.concatenate(
        [high, middle, low, jnp.zeros((LANES - 3 * ROWS, shards), F32)], axis=0
    )
    wide[pl.ds(2 * CAP, shards, stride=ROWS), :] = pieces.T
    wide[pl.ds(2 * CAP + 1, shards, stride=ROWS), :] = jnp.zeros((shards, LANES), F32)
    back_send[...] = wide[...].reshape(shards, ROWS, LANES).astype(BF16)

    def push_back(i, carry):
        pltpu.make_async_remote_copy(
            back_send.at[i],
            back.at[i],
            send_sem.at[1],
            recv_sem.at[1],
            device_id={"shard": peer(shards - i)},
            device_id_type=MESH,
        ).start()
        return carry

    lax.fori_loop(1, shards, push_back, 0)
    back[0] = back_send[0]
    others = back.at[pl.ds(1, shards - 1)]
    pltpu.make_async_copy(others, others, recv_sem.at[1]).wait()

    wide[...] = back[...].astype(F32).reshape(shards * ROWS, LANES)
    landed_rows = wide[...].astype(BF16)
    for half in range(2):
        enc_ref[:, half * LANES : (half + 1) * LANES] = lax.dot_general(
            place[half], landed_rows, TN, preferred_element_type=F32
        ).astype(BF16)
    pieces = rows_of(2 * CAP)
    sums = jnp.sum(pieces, axis=0, keepdims=True)
    sums = sums + pltpu.roll(sums, LANES - ROWS, 1) + pltpu.roll(sums, LANES - 2 * ROWS, 1)
    pair_total = jnp.maximum(sums[:, 7:8], 1.0)
    found = lax.dot_general(
        pieces.astype(BF16), named_f.astype(BF16), TN, preferred_element_type=F32
    )
    found = found[0:ROWS] + found[ROWS : 2 * ROWS] + found[2 * ROWS : 3 * ROWS]
    score_out = jnp.zeros((1, docs), F32)
    grad_out = jnp.zeros((1, docs), F32)
    for r in range(CAP):
        score_out = score_out + jnp.where(rank == r, found[r : r + 1], 0.0)
        grad_out = grad_out + jnp.where(rank == r, found[CAP + r : CAP + r + 1], 0.0)
    small_ref[0:1, :] = score_out
    small_ref[1:2, :] = grad_out / pair_total
    small_ref[2:3, :] = jnp.broadcast_to(sums[:, 6:7] / pair_total, (1, docs))
    small_ref[3:8, :] = jnp.zeros((5, docs), F32)

    for ref, at in ((send, 0), (back_send, 1)):
        sent = ref.at[pl.ds(1, shards - 1)]
        pltpu.make_async_copy(sent, sent, send_sem.at[at]).wait()


def body(
    features,
    owners,
    query_local,
    grades,
    query_weight,
    norm_gain,
    qkv_weight,
    out_weight,
    score_weight,
):
    shards = lax.axis_size("shard")
    heads = lax.axis_size("head")
    docs = features.shape[0]
    width, model = out_weight.shape
    slots = CAP * shards
    facts = jnp.stack([owners[:, 0], query_local, grades])
    vmem = pl.BlockSpec(memory_space=pltpu.VMEM)
    hbm = pl.BlockSpec(memory_space=pl.ANY)
    dma = pltpu.SemaphoreType.DMA
    blocks = pltpu.VMEM((shards, ROWS, LANES), BF16)
    encoded, small = pl.pallas_call(
        functools.partial(layer_kernel, shards, heads),
        out_shape=(
            jax.ShapeDtypeStruct((docs, width), BF16),
            jax.ShapeDtypeStruct((ROWS, docs), F32),
        ),
        in_specs=[vmem, vmem, vmem, vmem, hbm, hbm, vmem],
        out_specs=(vmem, vmem),
        scratch_shapes=[
            pltpu.VMEM((model, 3 * width), BF16),
            pltpu.VMEM((width, model), BF16),
            blocks,
            blocks,
            pltpu.VMEM((shards * ROWS, LANES), F32),
            pltpu.VMEM((heads, slots, width), BF16),
            pltpu.VMEM((slots, 3 * width), BF16),
            pltpu.VMEM((heads, slots, width), BF16),
            pltpu.VMEM((heads, slots, width), BF16),
            pltpu.VMEM((heads, ROWS, slots), F32),
            blocks,
            blocks,
            dma((2,)),
            dma((2,)),
            dma((2,)),
            dma((3, heads)),
            dma((3, heads)),
        ],
        compiler_params=pltpu.CompilerParams(
            collective_id=0, has_side_effects=True, vmem_limit_bytes=48 << 20
        ),
    )(
        features,
        facts,
        query_weight.reshape(1, -1),
        norm_gain.reshape(1, -1),
        qkv_weight.reshape(model, 3 * width),
        out_weight,
        score_weight.reshape(1, -1),
    )
    return encoded, small[0], small[1], small[2, 0]


def solution(mesh):
    placed = (
        P("shard", None),
        P("shard", None),
        P("shard"),
        P("shard"),
        P("shard"),
        P(),
        P(None, None, "head"),
        P("head", None),
        P("head"),
    )
    return jax.shard_map(
        body,
        mesh=mesh,
        in_specs=placed,
        out_specs=(P("shard", "head"), P("shard"), P("shard"), P()),
        check_vma=False,
    )
```

```python
import functools

import jax
import jax.numpy as jnp
from jax import lax
from jax.experimental import pallas as pl
from jax.experimental.pallas import tpu as pltpu
from jax.sharding import PartitionSpec as P

MESH = pl.DeviceIdType.MESH
HEAD_DIM = 64
CAP = 3
ROWS = 8
GROUPS = 4
LANES = 128
eps_norm = 1e-06
F32 = jnp.float32
BF16 = jnp.bfloat16
NT = (((1,), (1,)), ((), ()))
TN = (((0,), (0,)), ((), ()))


def dot(a, b):
    return jnp.dot(a, b, preferred_element_type=F32)


def iota(shape, dim):
    return lax.broadcasted_iota(jnp.int32, shape, dim)


def layer_kernel(
    shards,
    heads,
    feat_ref,
    doc_ref,
    qw_ref,
    gain_ref,
    wqkv_hbm,
    wout_hbm,
    sw_ref,
    enc_ref,
    small_ref,
    wqkv,
    wout,
    sw_all,
    send,
    recv,
    wide,
    gathered,
    proj,
    context,
    mixed_ref,
    back_send,
    back,
    score_send,
    score_recv,
    local_sem,
    send_sem,
    recv_sem,
    y_send,
    y_recv,
    pair_send,
    pair_recv,
):
    me = lax.axis_index("shard")
    head = lax.axis_index("head")
    docs = feat_ref.shape[0]
    width = wout_hbm.shape[0]
    model = wout_hbm.shape[1]
    slots = CAP * shards
    group = shards // GROUPS
    rows = CAP * group

    def peer(i):
        return lax.rem(me + i, shards)

    def head_peer(i):
        return lax.rem(head + i, heads)

    barrier = pltpu.get_barrier_semaphore()

    def greet(i, carry):
        pl.semaphore_signal(
            barrier, 1, device_id={"shard": peer(i)}, device_id_type=MESH
        )
        return carry

    lax.fori_loop(1, shards, greet, 0)
    for i in range(1, heads):
        pl.semaphore_signal(
            barrier, 1, device_id={"head": head_peer(i)}, device_id_type=MESH
        )
    load_qkv = pltpu.make_async_copy(wqkv_hbm, wqkv, local_sem.at[0])
    load_out = pltpu.make_async_copy(wout_hbm, wout.at[head], local_sem.at[1])
    load_qkv.start()
    load_out.start()

    owner = jnp.bitwise_and(doc_ref[0:1, :] - me, shards - 1)
    query = doc_ref[1:2, :].astype(F32) + 1.0
    grade = doc_ref[2:3, :].astype(F32)
    named = iota((shards, docs), 0) == owner
    named_f = named.astype(F32)
    earlier = (iota((docs, docs), 0) < iota((docs, docs), 1)).astype(F32).astype(BF16)
    before = dot(named_f.astype(BF16), earlier)
    rank_f = jnp.sum(before * named_f, axis=0, keepdims=True)
    rank = rank_f.astype(jnp.int32)
    first = owner * ROWS + 2 * rank
    block_row = iota((shards * ROWS, docs), 0)
    place = [
        (block_row == where).astype(F32).astype(BF16)
        for where in (first, first + 1, owner * ROWS + 2 * CAP)
    ]
    lane = iota((LANES, docs), 0)
    facts = jnp.where(lane == rank, query, 0.0) + jnp.where(
        lane == rank + CAP, grade, 0.0
    )
    left = pl.ds(pl.multiple_of(head * width, LANES), LANES)
    right = pl.ds(pl.multiple_of(head * width + LANES, LANES), LANES)
    block = dot(place[0], feat_ref[:, left]) + dot(place[1], feat_ref[:, right])
    block = block + lax.dot_general(
        place[2], facts.astype(BF16), NT, preferred_element_type=F32
    )
    send[...] = block.reshape(shards, ROWS, LANES).astype(BF16)
    sw_all[head] = jnp.broadcast_to(sw_ref[...], (ROWS, width))

    def exchange(source, target, step):
        copies = []
        for i in (2, 1, 3):
            copy = pltpu.make_async_remote_copy(
                source,
                target,
                y_send.at[step, i],
                y_recv.at[step, i],
                device_id={"head": head_peer(i)},
                device_id_type=MESH,
            )
            copy.start()
            copies.append(copy)
        return copies

    core = lax.rem(me, 2)
    half_rows = width // 2
    half = pl.ds(pl.multiple_of(core * half_rows, half_rows), half_rows)

    pl.semaphore_wait(barrier, shards - 1 + heads - 1)

    out_copies = exchange(wout_hbm.at[half], wout.at[head, half], 2 * GROUPS)
    sw_copies = exchange(sw_all.at[head], sw_all.at[head], 2 * GROUPS + 1)

    for g in range(GROUPS):

        def push(i, carry, g=g):
            pltpu.make_async_remote_copy(
                send.at[i],
                recv.at[i],
                send_sem.at[0],
                recv_sem.at[g],
                device_id={"shard": peer(i)},
                device_id_type=MESH,
            ).start()
            return carry

        lax.fori_loop(max(1, g * group), (g + 1) * group, push, 0)
    recv[0] = send[0]

    def arrived(ref, sem, g):
        low = max(1, g * group)
        some = ref.at[pl.ds(low, (g + 1) * group - low)]
        pltpu.make_async_copy(some, some, sem).wait()

    load_qkv.wait()
    load_out.wait()

    def slots_of(g):
        return pl.ds(g * rows, rows)

    def project(g, copies):
        for copy in copies:
            copy.wait()
        squares = jnp.zeros((rows, 1), F32)
        total = [jnp.zeros((rows, width), F32) for _ in range(3)]
        for k in range(heads):
            x = gathered[k, slots_of(g), :].astype(F32)
            squares = squares + jnp.sum(x * x, axis=1, keepdims=True)
            scaled = (x * gain_ref[:, k * width : (k + 1) * width]).astype(BF16)
            for j in range(3):
                total[j] = total[j] + dot(scaled, wqkv[j, k * width : (k + 1) * width])
        scale = lax.rsqrt(squares / model + eps_norm)
        for j in range(3):
            proj[slots_of(g), j * width : (j + 1) * width] = (
                total[j] * scale
            ).astype(BF16)

    fact_cols = []
    copies = []
    for g in range(GROUPS):
        arrived(recv, recv_sem.at[g], g)
        wide[...] = (
            recv[pl.ds(g * group, group)].astype(F32).reshape(group * ROWS, LANES)
        )
        for r in range(CAP):
            for k in range(2):
                gathered[
                    head,
                    g * rows + r * group : g * rows + (r + 1) * group,
                    k * LANES : (k + 1) * LANES,
                ] = wide[pl.ds(2 * r + k, group, stride=ROWS), :].astype(BF16)
        own = gathered.at[head, slots_of(g)]
        copies.append(exchange(own, own, g))
        fact_cols.append(wide[pl.ds(2 * CAP, group, stride=ROWS), :])
        if g >= 2:
            project(g - 2, copies[g - 2])

    diagonal = iota((slots, slots), 0) == iota((slots, slots), 1)

    def column(at):
        return jnp.concatenate(
            [f[:, at + r : at + r + 1] for f in fact_cols for r in range(CAP)], axis=0
        )

    def to_row(col):
        return jnp.sum(jnp.where(diagonal, col, 0.0), axis=0, keepdims=True)

    query_col, grade_col = column(0), column(CAP)
    query_row, grade_row = to_row(query_col), to_row(grade_col)
    related = (query_col == query_row) & (query_col > 0.5)
    bias = jnp.where(related | diagonal, 0.0, -jnp.inf)
    above = grade_col - grade_row
    counted = jnp.where(
        related & (above != 0.0), jnp.where(above > 0.0, 1.0, -1.0), 0.0
    )
    weight_col = jnp.zeros((slots, 1), F32)
    for k in range(qw_ref.shape[1]):
        weight_col = weight_col + jnp.where(
            query_col == float(k + 1), qw_ref[0:1, k : k + 1], 0.0
        )
    project(GROUPS - 2, copies[GROUPS - 2])

    for copy in out_copies + sw_copies:
        copy.wait()
    pair_copies = []
    for i in range(1, heads):
        piece = wout.at[lax.rem(head + heads - i, heads), half]
        copy = pltpu.make_async_remote_copy(
            piece,
            piece,
            pair_send.at[i],
            pair_recv.at[i],
            device_id={"shard": me + 1 - 2 * core},
            device_id_type=MESH,
        )
        copy.start()
        pair_copies.append(copy)
    project(GROUPS - 1, copies[GROUPS - 1])

    lane_col = iota((1, LANES), 1)
    copies = []
    for g in range(GROUPS):
        for pair in range(width // LANES):
            at = pair * LANES
            q2 = proj[slots_of(g), at : at + LANES]
            k2 = proj[:, width + at : width + at + LANES]
            v2 = proj[:, 2 * width + at : 2 * width + at + LANES]
            both_heads = None
            for sub in range(LANES // HEAD_DIM):
                mine = (lane_col // HEAD_DIM) == sub
                q1 = jnp.where(mine, q2, jnp.zeros_like(q2))
                scores = (
                    lax.dot_general(q1, k2, NT, preferred_element_type=F32)
                    * (HEAD_DIM**-0.5)
                    + bias[g * rows : (g + 1) * rows, :]
                )
                expo = jnp.exp(scores - jnp.max(scores, axis=1, keepdims=True))
                probs = (expo / jnp.sum(expo, axis=1, keepdims=True)).astype(BF16)
                out = dot(probs, v2)
                both_heads = out if sub == 0 else jnp.where(mine, out, both_heads)
            context[head, slots_of(g), at : at + LANES] = both_heads.astype(BF16)
        own = context.at[head, slots_of(g)]
        copies.append(exchange(own, own, GROUPS + g))
    for copy in pair_copies:
        copy.wait()

    own_cols = pl.ds(pl.multiple_of(head * width, width), width)
    score_cols = []
    for g in range(GROUPS):
        for copy in copies[g]:
            copy.wait()
        attended = dot(context[0, slots_of(g), :], wout[0])
        for k in range(1, heads):
            attended = attended + dot(context[k, slots_of(g), :], wout[k])
        squares = jnp.zeros((rows, 1), F32)
        weighted = jnp.zeros((rows, 1), F32)
        for k in range(heads):
            mixed = (
                gathered[k, slots_of(g), :].astype(F32)
                + attended[:, k * width : (k + 1) * width]
            )
            mixed_ref[:, k * width : (k + 1) * width] = mixed
            squares = squares + jnp.sum(mixed * mixed, axis=1, keepdims=True)
            weighted = weighted + jnp.sum(
                mixed * sw_all[k, 0:1, :], axis=1, keepdims=True
            )
        score_cols.append(weighted * lax.rsqrt(squares / model + eps_norm))
        encoded = mixed_ref[:, own_cols]
        for r in range(CAP):
            for k in range(2):
                wide[pl.ds(2 * r + k, group, stride=ROWS), :] = encoded[
                    r * group : (r + 1) * group, k * LANES : (k + 1) * LANES
                ]
        for k in range(2 * CAP, ROWS):
            wide[pl.ds(k, group, stride=ROWS), :] = jnp.zeros((group, LANES), F32)
        back_send[pl.ds(g * group, group)] = (
            wide[...].reshape(group, ROWS, LANES).astype(BF16)
        )

        def push_back(i, carry, g=g):
            pltpu.make_async_remote_copy(
                back_send.at[i],
                back.at[i],
                send_sem.at[1],
                recv_sem.at[GROUPS + g],
                device_id={"shard": peer(shards - i)},
                device_id_type=MESH,
            ).start()
            return carry

        lax.fori_loop(max(1, g * group), (g + 1) * group, push_back, 0)
    back[0] = back_send[0]

    score_col = jnp.concatenate(score_cols, axis=0)
    spread = counted * (to_row(score_col) - score_col)
    small = jnp.exp(-jnp.abs(spread))
    softplus = jnp.maximum(spread, 0.0) + jnp.log1p(small)
    sigmoid = jnp.where(spread >= 0.0, 1.0, small) / (1.0 + small)
    both = jnp.abs(counted)
    pull_col = -weight_col * jnp.sum(counted * sigmoid, axis=1, keepdims=True)
    pair_col = weight_col * jnp.sum(both * softplus, axis=1, keepdims=True)
    pair_sum = 0.5 * jnp.sum(pair_col, axis=0, keepdims=True)
    pair_count = 0.5 * jnp.sum(
        jnp.sum(both, axis=1, keepdims=True), axis=0, keepdims=True
    )

    def by_source(col, r):
        return jnp.concatenate(
            [
                col[g * rows + r * group : g * rows + (r + 1) * group]
                for g in range(GROUPS)
            ],
            axis=0,
        )

    words = [by_source(score_col, r) for r in range(CAP)]
    words += [by_source(pull_col, r) for r in range(CAP)]
    words += [pair_sum, pair_count]
    message = jnp.zeros((shards, LANES), F32)
    for k, word in enumerate(words):
        message = jnp.where(lane_col == k, word, message)
    score_send[...] = message.reshape(shards, 1, LANES)

    def push_scores(i, carry):
        pltpu.make_async_remote_copy(
            score_send.at[i],
            score_recv.at[i],
            send_sem.at[2],
            recv_sem.at[2 * GROUPS],
            device_id={"shard": peer(shards - i)},
            device_id_type=MESH,
        ).start()
        return carry

    lax.fori_loop(1, shards, push_scores, 0)
    score_recv[0] = score_send[0]

    placed = [jnp.zeros((docs, LANES), F32) for _ in range(2)]
    for g in range(GROUPS):
        arrived(back, recv_sem.at[GROUPS + g], g)
        landed = (
            back[pl.ds(g * group, group)]
            .astype(F32)
            .reshape(group * ROWS, LANES)
            .astype(BF16)
        )
        for k in range(2):
            placed[k] = placed[k] + lax.dot_general(
                place[k][g * group * ROWS : (g + 1) * group * ROWS],
                landed,
                TN,
                preferred_element_type=F32,
            )
    for k in range(2):
        enc_ref[:, k * LANES : (k + 1) * LANES] = placed[k].astype(BF16)
    others = score_recv.at[pl.ds(1, shards - 1)]
    pltpu.make_async_copy(others, others, recv_sem.at[2 * GROUPS]).wait()
    message = score_recv[...].reshape(shards, LANES)
    sums = jnp.sum(message, axis=0, keepdims=True)
    pair_total = jnp.maximum(sums[:, 7:8], 1.0)
    found = lax.dot_general(
        message,
        named_f,
        TN,
        precision=lax.Precision.HIGHEST,
        preferred_element_type=F32,
    )
    score_out = jnp.zeros((1, docs), F32)
    grad_out = jnp.zeros((1, docs), F32)
    for r in range(CAP):
        score_out = score_out + jnp.where(rank == r, found[r : r + 1], 0.0)
        grad_out = grad_out + jnp.where(rank == r, found[CAP + r : CAP + r + 1], 0.0)
    small_ref[0:1, :] = score_out
    small_ref[1:2, :] = grad_out / pair_total
    small_ref[2:3, :] = jnp.broadcast_to(sums[:, 6:7] / pair_total, (1, docs))
    small_ref[3:8, :] = jnp.zeros((5, docs), F32)

    for at, ref in enumerate((send, back_send, score_send)):
        sent = ref.at[pl.ds(1, shards - 1)]
        pltpu.make_async_copy(sent, sent, send_sem.at[at]).wait()


def body(
    features,
    owners,
    query_local,
    grades,
    query_weight,
    norm_gain,
    qkv_weight,
    out_weight,
    score_weight,
):
    shards = lax.axis_size("shard")
    heads = lax.axis_size("head")
    docs = features.shape[0]
    width, model = out_weight.shape
    slots = CAP * shards
    facts = jnp.stack([owners[:, 0], query_local, grades])
    vmem = pl.BlockSpec(memory_space=pltpu.VMEM)
    hbm = pl.BlockSpec(memory_space=pl.ANY)
    dma = pltpu.SemaphoreType.DMA
    blocks = pltpu.VMEM((shards, ROWS, LANES), BF16)
    encoded, small = pl.pallas_call(
        functools.partial(layer_kernel, shards, heads),
        out_shape=(
            jax.ShapeDtypeStruct((docs, width), BF16),
            jax.ShapeDtypeStruct((ROWS, docs), F32),
        ),
        in_specs=[vmem, vmem, vmem, vmem, hbm, hbm, vmem],
        out_specs=(vmem, vmem),
        scratch_shapes=[
            pltpu.VMEM((3, model, width), BF16),
            pltpu.VMEM((heads, width, model), BF16),
            pltpu.VMEM((heads, ROWS, width), F32),
            blocks,
            blocks,
            pltpu.VMEM((shards * ROWS // GROUPS, LANES), F32),
            pltpu.VMEM((heads, slots, width), BF16),
            pltpu.VMEM((slots, 3 * width), BF16),
            pltpu.VMEM((heads, slots, width), BF16),
            pltpu.VMEM((slots // GROUPS, model), F32),
            blocks,
            blocks,
            pltpu.VMEM((shards, 1, LANES), F32),
            pltpu.VMEM((shards, 1, LANES), F32),
            dma((2,)),
            dma((3,)),
            dma((2 * GROUPS + 1,)),
            dma((2 * GROUPS + 2, heads)),
            dma((2 * GROUPS + 2, heads)),
            dma((heads,)),
            dma((heads,)),
        ],
        compiler_params=pltpu.CompilerParams(
            collective_id=0, has_side_effects=True, vmem_limit_bytes=48 << 20
        ),
    )(
        features,
        facts,
        query_weight.reshape(1, -1),
        norm_gain.reshape(1, -1),
        jnp.transpose(qkv_weight, (1, 0, 2)),
        out_weight,
        score_weight.reshape(1, -1),
    )
    return encoded, small[0], small[1], small[2, 0]


def solution(mesh):
    placed = (
        P("shard", None),
        P("shard", None),
        P("shard"),
        P("shard"),
        P("shard"),
        P(),
        P(None, None, "head"),
        P("head", None),
        P("head"),
    )
    return jax.shard_map(
        body,
        mesh=mesh,
        in_specs=placed,
        out_specs=(P("shard", "head"), P("shard"), P("shard"), P()),
        check_vma=False,
    )
```

```python
import functools

import jax
import jax.numpy as jnp
from jax import lax
from jax.experimental import pallas as pl
from jax.experimental.pallas import tpu as pltpu
from jax.sharding import PartitionSpec as P

MESH = pl.DeviceIdType.MESH
HEAD_DIM = 64
CAP = 3
ROWS = 8
SIXTEENTHS = (4, 4, 4, 2, 2)
GROUPS = len(SIXTEENTHS)
LANES = 128
eps_norm = 1e-06
F32 = jnp.float32
BF16 = jnp.bfloat16
NT = (((1,), (1,)), ((), ()))
TN = (((0,), (0,)), ((), ()))


def dot(a, b):
    return jnp.dot(a, b, preferred_element_type=F32)


def iota(shape, dim):
    return lax.broadcasted_iota(jnp.int32, shape, dim)


def layer_kernel(
    shards,
    heads,
    query_count,
    feat_hbm,
    inputs_ref,
    wqkv_hbm,
    wout_hbm,
    enc_ref,
    small_ref,
    feat_ref,
    wqkv,
    wout,
    sw_all,
    send,
    recv,
    facts_send,
    facts_recv,
    spread_rows,
    gathered,
    proj,
    context,
    mixed_ref,
    back_send,
    back,
    score_send,
    score_recv,
    local_sem,
    send_sem,
    recv_sem,
    y_send,
    y_recv,
    pair_send,
    pair_recv,
    facts_sent,
    facts_came,
    facts_y_sent,
    facts_y_came,
):
    me = lax.axis_index("shard")
    head = lax.axis_index("head")
    docs = feat_hbm.shape[0]
    width = wout_hbm.shape[0]
    model = wout_hbm.shape[1]
    slots = CAP * shards
    cut = [shards * sum(SIXTEENTHS[:g]) // 16 for g in range(GROUPS + 1)]
    share = shards // heads

    def in_halves(x):
        return jnp.stack([x[:, :LANES], x[:, LANES:]], axis=1).astype(BF16)

    def halves_of(ref, g):
        x = ref[slots_of(g)].astype(F32)
        return [x[:, k, :].astype(BF16) for k in range(2)]

    def slots_of(g):
        return slice(cut[g] * CAP, cut[g + 1] * CAP)

    def peer(i):
        return lax.rem(me + i, shards)

    def head_peer(i):
        return lax.rem(head + i, heads)

    cols = pl.ds(pl.multiple_of(head * width, width), width)
    arguments = (
        (feat_hbm.at[:, cols], feat_ref),
        (wqkv_hbm, wqkv),
        (wout_hbm, wout.at[head]),
    )
    loads = [
        pltpu.make_async_copy(source, target, local_sem.at[k])
        for k, (source, target) in enumerate(arguments)
    ]
    for load in loads:
        load.start()

    barrier = pltpu.get_barrier_semaphore()

    def greet(i, carry):
        pl.semaphore_signal(
            barrier, 1, device_id={"shard": peer(i)}, device_id_type=MESH
        )
        return carry

    lax.fori_loop(1, shards, greet, 0, unroll=True)
    for i in range(1, heads):
        pl.semaphore_signal(
            barrier, 1, device_id={"head": head_peer(i)}, device_id_type=MESH
        )

    owner = jnp.bitwise_and(
        inputs_ref[0:1, :docs].astype(jnp.int32) - me, shards - 1
    )
    query = inputs_ref[1:2, :docs] + 1.0
    grade = inputs_ref[2:3, :docs]
    named = iota((shards, docs), 0) == owner
    named_f = named.astype(F32)
    earlier = (iota((docs, docs), 0) < iota((docs, docs), 1)).astype(F32).astype(BF16)
    before = dot(named_f.astype(BF16), earlier)
    rank_f = jnp.sum(before * named_f, axis=0, keepdims=True)
    rank = rank_f.astype(jnp.int32)
    place = (iota((slots, docs), 0) == owner * CAP + rank).astype(F32).astype(BF16)
    lane = iota((LANES, docs), 0)
    facts = jnp.where(lane == rank, query, 0.0) + jnp.where(
        lane == rank + CAP, grade, 0.0
    )
    loads[0].wait()
    block = dot(place, feat_ref[...])
    send[...] = in_halves(block)
    facts_send[...] = lax.dot_general(
        named_f.astype(BF16), facts.astype(BF16), NT, preferred_element_type=F32
    ).reshape(shards, 1, LANES)
    sw_all[head] = jnp.broadcast_to(inputs_ref[3:4, :width], (ROWS, width))

    def exchange(source, target, step):
        copies = []
        for i in (2, 1, 3):
            copy = pltpu.make_async_remote_copy(
                source,
                target,
                y_send.at[step, i],
                y_recv.at[step, i],
                device_id={"head": head_peer(i)},
                device_id_type=MESH,
            )
            copy.start()
            copies.append(copy)
        return copies

    core = lax.rem(me, 2)
    half_rows = width // 2
    half = pl.ds(pl.multiple_of(core * half_rows, half_rows), half_rows)

    pl.semaphore_wait(barrier, shards - 1 + heads - 1)

    out_copies = exchange(wout_hbm.at[half], wout.at[head, half], 2 * GROUPS)
    sw_copies = exchange(sw_all.at[head], sw_all.at[head], 2 * GROUPS + 1)

    def push_facts(i, carry):
        pltpu.make_async_remote_copy(
            facts_send.at[i],
            facts_recv.at[i],
            facts_sent,
            facts_came,
            device_id={"shard": peer(i)},
            device_id_type=MESH,
        ).start()
        return carry

    for g in range(heads):

        @pl.when(head == g)
        def _(g=g):
            lax.fori_loop(max(1, g * share), (g + 1) * share, push_facts, 0)

    for g in range(GROUPS):

        def push(i, carry, g=g):
            at = pl.ds(i * CAP, CAP)
            pltpu.make_async_remote_copy(
                send.at[at],
                recv.at[at],
                send_sem.at[0],
                recv_sem.at[g],
                device_id={"shard": peer(i)},
                device_id_type=MESH,
            ).start()
            return carry

        lax.fori_loop(max(1, cut[g]), cut[g + 1], push, 0)
    recv[0:CAP] = send[0:CAP]

    def arrived(ref, sem, g):
        low = max(1, cut[g]) * CAP
        some = ref.at[pl.ds(low, cut[g + 1] * CAP - low)]
        pltpu.make_async_copy(some, some, sem).wait()

    def share_facts(g):
        low = max(1, g * share)
        got = facts_recv.at[pl.ds(low, (g + 1) * share - low)]
        all_of = facts_recv.at[pl.ds(g * share, share)]
        mine = head == g

        def to(i):
            return pltpu.make_async_remote_copy(
                all_of,
                all_of,
                facts_y_sent.at[i],
                facts_y_came.at[g],
                device_id={"head": head_peer(i)},
                device_id_type=MESH,
            )

        @pl.when(mine)
        def _():
            if g == 0:
                facts_recv[0] = facts_send[0]
            pltpu.make_async_copy(got, got, facts_came).wait()
            for i in (2, 1, 3):
                to(i).start()

        def finish():
            @pl.when(mine)
            def _():
                for i in (2, 1, 3):
                    to(i).wait_send()
                sent = facts_send.at[pl.ds(low, (g + 1) * share - low)]
                pltpu.make_async_copy(sent, sent, facts_sent).wait()

            @pl.when(jnp.logical_not(mine))
            def _():
                to(1).wait_recv()

        return finish

    for load in loads[1:]:
        load.wait()

    def project(g, copies):
        for copy in copies:
            copy.wait()
        rows = (cut[g + 1] - cut[g]) * CAP
        squares = jnp.zeros((rows, 1), F32)
        total = [jnp.zeros((rows, width), F32) for _ in range(3)]
        for k in range(heads):
            x = gathered[k, slots_of(g), :].astype(F32)
            squares = squares + jnp.sum(x * x, axis=1, keepdims=True)
            scaled = (x * inputs_ref[4:5, k * width : (k + 1) * width]).astype(BF16)
            for j in range(3):
                total[j] = total[j] + dot(scaled, wqkv[j, k * width : (k + 1) * width])
        scale = lax.rsqrt(squares / model + eps_norm)
        for j in range(3):
            proj[slots_of(g), j * width : (j + 1) * width] = (
                total[j] * scale
            ).astype(BF16)

    copies = []
    finish_facts = [share_facts(g) for g in range(heads)]
    for g in range(GROUPS):
        arrived(recv, recv_sem.at[g], g)
        for k, part in enumerate(halves_of(recv, g)):
            gathered[head, slots_of(g), k * LANES : (k + 1) * LANES] = part
        own = gathered.at[head, slots_of(g)]
        copies.append(exchange(own, own, g))
        if g == 1:
            for finish in finish_facts:
                finish()
            lane_col = iota((1, LANES), 1)
            facts = facts_recv[...].reshape(shards, LANES)
            for r in range(CAP):
                spread_rows[pl.ds(r, shards, stride=CAP), :] = jnp.where(
                    lane_col == 0, facts[:, r : r + 1], facts[:, CAP + r : CAP + r + 1]
                )
            diagonal = iota((slots, slots), 0) == iota((slots, slots), 1)

            def to_row(col):
                return jnp.sum(jnp.where(diagonal, col, 0.0), axis=0, keepdims=True)

            query_col, grade_col = spread_rows[:, 0:1], spread_rows[:, 1:2]
            query_row, grade_row = to_row(query_col), to_row(grade_col)
            related = (query_col == query_row) & (query_col > 0.5)
            bias = jnp.where(related | diagonal, 0.0, -jnp.inf)
            above = grade_col - grade_row
            counted = jnp.where(
                related & (above != 0.0), jnp.where(above > 0.0, 1.0, -1.0), 0.0
            )
            weight_col = jnp.zeros((slots, 1), F32)
            for k in range(query_count):
                weight_col = weight_col + jnp.where(
                    query_col == float(k + 1), inputs_ref[5:6, k : k + 1], 0.0
                )
        if g >= 2:
            project(g - 2, copies[g - 2])
    project(GROUPS - 2, copies[GROUPS - 2])

    for copy in out_copies + sw_copies:
        copy.wait()
    pair_copies = []
    for i in range(1, heads):
        piece = wout.at[lax.rem(head + heads - i, heads), half]
        copy = pltpu.make_async_remote_copy(
            piece,
            piece,
            pair_send.at[i],
            pair_recv.at[i],
            device_id={"shard": me + 1 - 2 * core},
            device_id_type=MESH,
        )
        copy.start()
        pair_copies.append(copy)
    project(GROUPS - 1, copies[GROUPS - 1])

    copies = []
    for g in range(GROUPS):
        for pair in range(width // LANES):
            at = pair * LANES
            q2 = proj[slots_of(g), at : at + LANES]
            k2 = proj[:, width + at : width + at + LANES]
            v2 = proj[:, 2 * width + at : 2 * width + at + LANES]
            both_heads = None
            for sub in range(LANES // HEAD_DIM):
                mine = (lane_col // HEAD_DIM) == sub
                q1 = jnp.where(mine, q2, jnp.zeros_like(q2))
                scores = (
                    lax.dot_general(q1, k2, NT, preferred_element_type=F32)
                    * (HEAD_DIM**-0.5)
                    + bias[slots_of(g), :]
                )
                expo = jnp.exp(scores - jnp.max(scores, axis=1, keepdims=True))
                probs = (expo / jnp.sum(expo, axis=1, keepdims=True)).astype(BF16)
                out = dot(probs, v2)
                both_heads = out if sub == 0 else jnp.where(mine, out, both_heads)
            context[head, slots_of(g), at : at + LANES] = both_heads.astype(BF16)
        own = context.at[head, slots_of(g)]
        copies.append(exchange(own, own, GROUPS + g))
    for copy in pair_copies:
        copy.wait()

    score_cols = []
    for g in range(GROUPS):
        for copy in copies[g]:
            copy.wait()
        attended = dot(context[0, slots_of(g), :], wout[0])
        for k in range(1, heads):
            attended = attended + dot(context[k, slots_of(g), :], wout[k])
        rows = (cut[g + 1] - cut[g]) * CAP
        squares = jnp.zeros((rows, 1), F32)
        weighted = jnp.zeros((rows, 1), F32)
        for k in range(heads):
            mixed = (
                gathered[k, slots_of(g), :].astype(F32)
                + attended[:, k * width : (k + 1) * width]
            )
            mixed_ref[0:rows, k * width : (k + 1) * width] = mixed
            squares = squares + jnp.sum(mixed * mixed, axis=1, keepdims=True)
            weighted = weighted + jnp.sum(
                mixed * sw_all[k, 0:1, :], axis=1, keepdims=True
            )
        score_cols.append(weighted * lax.rsqrt(squares / model + eps_norm))
        back_send[slots_of(g)] = in_halves(mixed_ref[0:rows, cols])

        def push_back(i, carry, g=g):
            at = pl.ds(i * CAP, CAP)
            pltpu.make_async_remote_copy(
                back_send.at[at],
                back.at[at],
                send_sem.at[1],
                recv_sem.at[GROUPS + g],
                device_id={"shard": peer(shards - i)},
                device_id_type=MESH,
            ).start()
            return carry

        lax.fori_loop(
            max(1, cut[g]), cut[g + 1], push_back, 0, unroll=g == GROUPS - 1
        )
    back[0:CAP] = back_send[0:CAP]

    score_col = jnp.concatenate(score_cols, axis=0)
    spread = counted * (to_row(score_col) - score_col)
    small = jnp.exp(-jnp.abs(spread))
    softplus = jnp.maximum(spread, 0.0) + jnp.log1p(small)
    sigmoid = jnp.where(spread >= 0.0, 1.0, small) / (1.0 + small)
    both = jnp.abs(counted)
    pull_col = -weight_col * jnp.sum(counted * sigmoid, axis=1, keepdims=True)
    pair_col = weight_col * jnp.sum(both * softplus, axis=1, keepdims=True)
    pair_sum = 0.5 * jnp.sum(pair_col, axis=0, keepdims=True)
    pair_count = 0.5 * jnp.sum(
        jnp.sum(both, axis=1, keepdims=True), axis=0, keepdims=True
    )

    spread_rows[...] = jnp.where(lane_col == 0, score_col, pull_col)
    by_rank = [spread_rows[pl.ds(r, shards, stride=CAP), :] for r in range(CAP)]
    words = [x[:, 0:1] for x in by_rank] + [x[:, 1:2] for x in by_rank]
    words += [pair_sum, pair_count]
    message = jnp.zeros((shards, LANES), F32)
    for k, word in enumerate(words):
        message = jnp.where(lane_col == k, word, message)
    score_send[...] = message.reshape(shards, 1, LANES)

    def push_scores(i, carry):
        pltpu.make_async_remote_copy(
            score_send.at[i],
            score_recv.at[i],
            send_sem.at[2],
            recv_sem.at[2 * GROUPS],
            device_id={"shard": peer(shards - i)},
            device_id_type=MESH,
        ).start()
        return carry

    lax.fori_loop(1, shards, push_scores, 0)
    score_recv[0] = score_send[0]

    placed = [jnp.zeros((docs, LANES), F32) for _ in range(2)]
    for g in range(GROUPS):
        arrived(back, recv_sem.at[GROUPS + g], g)
        for k, part in enumerate(halves_of(back, g)):
            placed[k] = placed[k] + lax.dot_general(
                place[slots_of(g)],
                part,
                TN,
                preferred_element_type=F32,
            )
    for k in range(2):
        enc_ref[:, k * LANES : (k + 1) * LANES] = placed[k].astype(BF16)
    others = score_recv.at[pl.ds(1, shards - 1)]
    pltpu.make_async_copy(others, others, recv_sem.at[2 * GROUPS]).wait()
    message = score_recv[...].reshape(shards, LANES)
    sums = jnp.sum(message, axis=0, keepdims=True)
    pair_total = jnp.maximum(sums[:, 7:8], 1.0)
    found = lax.dot_general(
        message,
        named_f,
        TN,
        precision=lax.Precision.HIGHEST,
        preferred_element_type=F32,
    )
    score_out = jnp.zeros((1, docs), F32)
    grad_out = jnp.zeros((1, docs), F32)
    for r in range(CAP):
        score_out = score_out + jnp.where(rank == r, found[r : r + 1], 0.0)
        grad_out = grad_out + jnp.where(rank == r, found[CAP + r : CAP + r + 1], 0.0)
    small_ref[0:1, :] = score_out
    small_ref[1:2, :] = grad_out / pair_total
    small_ref[2:3, :] = jnp.broadcast_to(sums[:, 6:7] / pair_total, (1, docs))
    small_ref[3:8, :] = jnp.zeros((5, docs), F32)

    for at, ref in enumerate((send, back_send, score_send)):
        first = 1 if ref is score_send else CAP
        sent = ref.at[pl.ds(first, ref.shape[0] - first)]
        pltpu.make_async_copy(sent, sent, send_sem.at[at]).wait()


def body(
    features,
    owners,
    query_local,
    grades,
    query_weight,
    norm_gain,
    qkv_weight,
    out_weight,
    score_weight,
):
    shards = lax.axis_size("shard")
    heads = lax.axis_size("head")
    docs = features.shape[0]
    width, model = out_weight.shape
    slots = CAP * shards
    vmem = pl.BlockSpec(memory_space=pltpu.VMEM)
    hbm = pl.BlockSpec(memory_space=pltpu.HBM)
    dma = pltpu.SemaphoreType.DMA
    def row(x, at):
        return jnp.pad(
            x.reshape(1, -1), ((at, ROWS - 1 - at), (0, model - x.size))
        )

    integers = row(owners, 0) + row(query_local, 1) + row(grades, 2)
    floats = row(score_weight, 3) + row(norm_gain, 4) + row(query_weight, 5)
    small = integers.astype(F32) + floats
    blocks = pltpu.VMEM((slots, 2, LANES), BF16)
    words = pltpu.VMEM((shards, 1, LANES), F32)
    encoded, back_small = pl.pallas_call(
        functools.partial(layer_kernel, shards, heads, query_weight.shape[0]),
        out_shape=(
            jax.ShapeDtypeStruct((docs, width), BF16),
            jax.ShapeDtypeStruct((ROWS, docs), F32),
        ),
        in_specs=[hbm, vmem, hbm, hbm],
        out_specs=(vmem, vmem),
        scratch_shapes=[
            pltpu.VMEM((docs, width), BF16),
            pltpu.VMEM((3, model, width), BF16),
            pltpu.VMEM((heads, width, model), BF16),
            pltpu.VMEM((heads, ROWS, width), F32),
            blocks,
            blocks,
            words,
            words,
            pltpu.VMEM((slots, LANES), F32),
            pltpu.VMEM((heads, slots, width), BF16),
            pltpu.VMEM((slots, 3 * width), BF16),
            pltpu.VMEM((heads, slots, width), BF16),
            pltpu.VMEM((slots * max(SIXTEENTHS) // 16, model), F32),
            blocks,
            blocks,
            words,
            words,
            dma((3,)),
            dma((3,)),
            dma((2 * GROUPS + 1,)),
            dma((2 * GROUPS + 2, heads)),
            dma((2 * GROUPS + 2, heads)),
            dma((heads,)),
            dma((heads,)),
            dma,
            dma,
            dma((heads,)),
            dma((heads,)),
        ],
        compiler_params=pltpu.CompilerParams(
            collective_id=0, has_side_effects=True, vmem_limit_bytes=107 << 19
        ),
    )(
        features,
        small,
        jnp.transpose(qkv_weight, (1, 0, 2)),
        out_weight,
    )
    return encoded, back_small[0], back_small[1], back_small[2, 0]


def solution(mesh):
    placed = (
        P("shard", None),
        P("shard", None),
        P("shard"),
        P("shard"),
        P("shard"),
        P(),
        P(None, None, "head"),
        P("head", None),
        P("head"),
    )
    return jax.shard_map(
        body,
        mesh=mesh,
        in_specs=placed,
        out_specs=(P("shard", "head"), P("shard"), P("shard"), P()),
        check_vma=False,
    )
```

```python
import functools

import jax
import jax.numpy as jnp
from jax import lax
from jax.experimental import pallas as pl
from jax.experimental.pallas import tpu as pltpu
from jax.sharding import PartitionSpec as P

MESH = pl.DeviceIdType.MESH
HEAD_DIM = 64
CAP = 3
ROWS = 8
SIXTEENTHS = (4, 4, 4, 2, 2)
GROUPS = len(SIXTEENTHS)
LANES = 128
eps_norm = 1e-06
F32 = jnp.float32
BF16 = jnp.bfloat16
NT = (((1,), (1,)), ((), ()))
TN = (((0,), (0,)), ((), ()))


def dot(a, b):
    return jnp.dot(a, b, preferred_element_type=F32)


def iota(shape, dim):
    return lax.broadcasted_iota(jnp.int32, shape, dim)


def layer_kernel(
    shards,
    heads,
    query_count,
    feat_hbm,
    inputs_ref,
    wqkv_hbm,
    wout_hbm,
    enc_ref,
    small_ref,
    feat_ref,
    wqkv,
    wout,
    sw_all,
    send,
    recv,
    facts_send,
    facts_recv,
    spread_rows,
    gathered,
    proj,
    context,
    mixed_ref,
    back_send,
    back,
    score_send,
    score_recv,
    local_sem,
    send_sem,
    recv_sem,
    y_send,
    y_recv,
    pair_send,
    pair_recv,
    facts_sent,
    facts_came,
    facts_y_sent,
    facts_y_came,
):
    me = lax.axis_index("shard")
    head = lax.axis_index("head")
    docs = feat_hbm.shape[0]
    width = wout_hbm.shape[0]
    model = wout_hbm.shape[1]
    slots = CAP * shards
    cut = [shards * sum(SIXTEENTHS[:g]) // 16 for g in range(GROUPS + 1)]
    share = shards // heads

    def in_halves(x):
        return jnp.stack([x[:, :LANES], x[:, LANES:]], axis=1).astype(BF16)

    def halves_of(ref, g):
        x = ref[slots_of(g)].astype(F32)
        return [x[:, k, :].astype(BF16) for k in range(2)]

    def slots_of(g):
        return slice(cut[g] * CAP, cut[g + 1] * CAP)

    def peer(i):
        return lax.rem(me + i, shards)

    def head_peer(i):
        return lax.rem(head + i, heads)

    cols = pl.ds(pl.multiple_of(head * width, width), width)
    arguments = (
        (feat_hbm.at[:, cols], feat_ref),
        (wqkv_hbm, wqkv),
        (wout_hbm, wout.at[head]),
    )
    loads = [
        pltpu.make_async_copy(source, target, local_sem.at[k])
        for k, (source, target) in enumerate(arguments)
    ]
    for load in loads:
        load.start()

    barrier = pltpu.get_barrier_semaphore()

    def greet(i, carry):
        pl.semaphore_signal(
            barrier, 1, device_id={"shard": peer(i)}, device_id_type=MESH
        )
        return carry

    lax.fori_loop(1, shards, greet, 0, unroll=True)
    for i in range(1, heads):
        pl.semaphore_signal(
            barrier, 1, device_id={"head": head_peer(i)}, device_id_type=MESH
        )

    owner = jnp.bitwise_and(
        inputs_ref[0:1, :docs].astype(jnp.int32) - me, shards - 1
    )
    query = inputs_ref[1:2, :docs] + 1.0
    grade = inputs_ref[2:3, :docs]
    named = iota((shards, docs), 0) == owner
    named_f = named.astype(F32)
    earlier = (iota((docs, docs), 0) < iota((docs, docs), 1)).astype(F32).astype(BF16)
    before = dot(named_f.astype(BF16), earlier)
    rank_f = jnp.sum(before * named_f, axis=0, keepdims=True)
    rank = rank_f.astype(jnp.int32)
    place = (iota((slots, docs), 0) == owner * CAP + rank).astype(F32).astype(BF16)
    lane = iota((LANES, docs), 0)
    facts = jnp.where(lane == rank, query, 0.0) + jnp.where(
        lane == rank + CAP, grade, 0.0
    )
    loads[0].wait()
    block = dot(place, feat_ref[...])
    send[...] = in_halves(block)
    facts_send[...] = lax.dot_general(
        named_f.astype(BF16), facts.astype(BF16), NT, preferred_element_type=F32
    ).reshape(shards, 1, LANES)
    sw_all[head] = jnp.broadcast_to(inputs_ref[3:4, :width], (ROWS, width))

    def exchange(source, target, step):
        copies = []
        for i in (2, 1, 3):
            copy = pltpu.make_async_remote_copy(
                source,
                target,
                y_send.at[step, i],
                y_recv.at[step, i],
                device_id={"head": head_peer(i)},
                device_id_type=MESH,
            )
            copy.start()
            copies.append(copy)
        return copies

    core = lax.rem(me, 2)
    half_rows = width // 2
    half = pl.ds(pl.multiple_of(core * half_rows, half_rows), half_rows)

    pl.semaphore_wait(barrier, shards - 1 + heads - 1)

    out_copies = exchange(wout_hbm.at[half], wout.at[head, half], 2 * GROUPS)
    sw_copies = exchange(sw_all.at[head], sw_all.at[head], 2 * GROUPS + 1)

    def push_facts(i, carry):
        pltpu.make_async_remote_copy(
            facts_send.at[i],
            facts_recv.at[i],
            facts_sent,
            facts_came,
            device_id={"shard": peer(i)},
            device_id_type=MESH,
        ).start()
        return carry

    for g in range(heads):

        @pl.when(head == g)
        def _(g=g):
            lax.fori_loop(max(1, g * share), (g + 1) * share, push_facts, 0)

    for g in range(GROUPS):

        def push(i, carry, g=g):
            at = pl.ds(i * CAP, CAP)
            pltpu.make_async_remote_copy(
                send.at[at],
                recv.at[at],
                send_sem.at[0],
                recv_sem.at[g],
                device_id={"shard": peer(i)},
                device_id_type=MESH,
            ).start()
            return carry

        lax.fori_loop(max(1, cut[g]), cut[g + 1], push, 0)
    recv[0:CAP] = send[0:CAP]

    def arrived(ref, sem, g):
        low = max(1, cut[g]) * CAP
        some = ref.at[pl.ds(low, cut[g + 1] * CAP - low)]
        pltpu.make_async_copy(some, some, sem).wait()

    def share_facts(g):
        low = max(1, g * share)
        got = facts_recv.at[pl.ds(low, (g + 1) * share - low)]
        all_of = facts_recv.at[pl.ds(g * share, share)]
        mine = head == g

        def to(i):
            return pltpu.make_async_remote_copy(
                all_of,
                all_of,
                facts_y_sent.at[i],
                facts_y_came.at[g],
                device_id={"head": head_peer(i)},
                device_id_type=MESH,
            )

        @pl.when(mine)
        def _():
            if g == 0:
                facts_recv[0] = facts_send[0]
            pltpu.make_async_copy(got, got, facts_came).wait()
            for i in (2, 1, 3):
                to(i).start()

        def finish():
            @pl.when(mine)
            def _():
                for i in (2, 1, 3):
                    to(i).wait_send()
                sent = facts_send.at[pl.ds(low, (g + 1) * share - low)]
                pltpu.make_async_copy(sent, sent, facts_sent).wait()

            @pl.when(jnp.logical_not(mine))
            def _():
                to(1).wait_recv()

        return finish

    for load in loads[1:]:
        load.wait()

    def project(g, copies):
        for copy in copies:
            copy.wait()
        rows = (cut[g + 1] - cut[g]) * CAP
        squares = jnp.zeros((rows, 1), F32)
        total = [jnp.zeros((rows, width), F32) for _ in range(3)]
        for k in range(heads):
            x = gathered[k, slots_of(g), :].astype(F32)
            squares = squares + jnp.sum(x * x, axis=1, keepdims=True)
            scaled = (x * inputs_ref[4:5, k * width : (k + 1) * width]).astype(BF16)
            for j in range(3):
                total[j] = total[j] + dot(scaled, wqkv[j, k * width : (k + 1) * width])
        scale = lax.rsqrt(squares / model + eps_norm)
        for j in range(3):
            proj[slots_of(g), j * width : (j + 1) * width] = (
                total[j] * scale
            ).astype(BF16)

    copies = []
    finish_facts = [share_facts(g) for g in range(heads)]
    for g in range(GROUPS):
        arrived(recv, recv_sem.at[g], g)
        for k, part in enumerate(halves_of(recv, g)):
            gathered[head, slots_of(g), k * LANES : (k + 1) * LANES] = part
        own = gathered.at[head, slots_of(g)]
        copies.append(exchange(own, own, g))
        if g == 1:
            for finish in finish_facts:
                finish()
            lane_col = iota((1, LANES), 1)
            facts = facts_recv[...].reshape(shards, LANES)
            for r in range(CAP):
                spread_rows[pl.ds(r, shards, stride=CAP), :] = jnp.where(
                    lane_col == 0, facts[:, r : r + 1], facts[:, CAP + r : CAP + r + 1]
                )
            diagonal = iota((slots, slots), 0) == iota((slots, slots), 1)

            def to_row(col):
                return jnp.sum(jnp.where(diagonal, col, 0.0), axis=0, keepdims=True)

            query_col, grade_col = spread_rows[:, 0:1], spread_rows[:, 1:2]
            query_row, grade_row = to_row(query_col), to_row(grade_col)
            related = (query_col == query_row) & (query_col > 0.5)
            bias = jnp.where(related | diagonal, 0.0, -jnp.inf)
            above = grade_col - grade_row
            counted = jnp.where(
                related & (above != 0.0), jnp.where(above > 0.0, 1.0, -1.0), 0.0
            )
            weight_col = jnp.zeros((slots, 1), F32)
            for k in range(query_count):
                weight_col = weight_col + jnp.where(
                    query_col == float(k + 1), inputs_ref[5:6, k : k + 1], 0.0
                )
        if g >= 2:
            project(g - 2, copies[g - 2])
    project(GROUPS - 2, copies[GROUPS - 2])

    for copy in out_copies + sw_copies:
        copy.wait()
    pair_copies = []
    for i in range(1, heads):
        piece = wout.at[lax.rem(head + heads - i, heads), half]
        copy = pltpu.make_async_remote_copy(
            piece,
            piece,
            pair_send.at[i],
            pair_recv.at[i],
            device_id={"shard": me + 1 - 2 * core},
            device_id_type=MESH,
        )
        copy.start()
        pair_copies.append(copy)
    project(GROUPS - 1, copies[GROUPS - 1])

    keys_t = proj[:, width : 2 * width].T
    copies = []
    for g in range(GROUPS):
        for pair in range(width // LANES):
            at = pair * LANES
            q2 = proj[slots_of(g), at : at + LANES] * jnp.asarray(HEAD_DIM**-0.5, BF16)
            k2 = keys_t[at : at + LANES, :]
            v2 = proj[:, 2 * width + at : 2 * width + at + LANES]
            halves = [
                jnp.where((lane_col // HEAD_DIM) == sub, q2, jnp.zeros_like(q2))
                for sub in range(LANES // HEAD_DIM)
            ]
            scores = dot(jnp.concatenate(halves, axis=0), k2) + jnp.concatenate(
                [bias[slots_of(g), :]] * 2, axis=0
            )
            expo = jnp.exp(scores - jnp.max(scores, axis=1, keepdims=True))
            whole = 1.0 / jnp.sum(expo, axis=1, keepdims=True)
            out = dot(expo.astype(BF16), v2) * whole
            rows = (cut[g + 1] - cut[g]) * CAP
            both_heads = jnp.where(lane_col < HEAD_DIM, out[:rows], out[rows:])
            context[head, slots_of(g), at : at + LANES] = both_heads.astype(BF16)
        own = context.at[head, slots_of(g)]
        copies.append(exchange(own, own, GROUPS + g))
    for copy in pair_copies:
        copy.wait()

    score_cols = []
    for g in range(GROUPS):
        for copy in copies[g]:
            copy.wait()
        attended = dot(context[0, slots_of(g), :], wout[0])
        for k in range(1, heads):
            attended = attended + dot(context[k, slots_of(g), :], wout[k])
        rows = (cut[g + 1] - cut[g]) * CAP
        squares = jnp.zeros((rows, 1), F32)
        weighted = jnp.zeros((rows, 1), F32)
        for k in range(heads):
            mixed = (
                gathered[k, slots_of(g), :].astype(F32)
                + attended[:, k * width : (k + 1) * width]
            )
            mixed_ref[0:rows, k * width : (k + 1) * width] = mixed
            squares = squares + jnp.sum(mixed * mixed, axis=1, keepdims=True)
            weighted = weighted + jnp.sum(
                mixed * sw_all[k, 0:1, :], axis=1, keepdims=True
            )
        score_cols.append(weighted * lax.rsqrt(squares / model + eps_norm))
        back_send[slots_of(g)] = in_halves(mixed_ref[0:rows, cols])

        def push_back(i, carry, g=g):
            at = pl.ds(i * CAP, CAP)
            pltpu.make_async_remote_copy(
                back_send.at[at],
                back.at[at],
                send_sem.at[1],
                recv_sem.at[GROUPS + g],
                device_id={"shard": peer(shards - i)},
                device_id_type=MESH,
            ).start()
            return carry

        lax.fori_loop(
            max(1, cut[g]), cut[g + 1], push_back, 0, unroll=g == GROUPS - 1
        )
    back[0:CAP] = back_send[0:CAP]

    score_col = jnp.concatenate(score_cols, axis=0)
    spread = counted * (to_row(score_col) - score_col)
    small = jnp.exp(-jnp.abs(spread))
    softplus = jnp.maximum(spread, 0.0) + jnp.log1p(small)
    sigmoid = jnp.where(spread >= 0.0, 1.0, small) / (1.0 + small)
    both = jnp.abs(counted)
    pull_col = -weight_col * jnp.sum(counted * sigmoid, axis=1, keepdims=True)
    pair_col = weight_col * jnp.sum(both * softplus, axis=1, keepdims=True)
    pair_sum = 0.5 * jnp.sum(pair_col, axis=0, keepdims=True)
    pair_count = 0.5 * jnp.sum(
        jnp.sum(both, axis=1, keepdims=True), axis=0, keepdims=True
    )

    spread_rows[...] = jnp.where(lane_col == 0, score_col, pull_col)
    by_rank = [spread_rows[pl.ds(r, shards, stride=CAP), :] for r in range(CAP)]
    words = [x[:, 0:1] for x in by_rank] + [x[:, 1:2] for x in by_rank]
    words += [pair_sum, pair_count]
    message = jnp.zeros((shards, LANES), F32)
    for k, word in enumerate(words):
        message = jnp.where(lane_col == k, word, message)
    score_send[...] = message.reshape(shards, 1, LANES)

    def push_scores(i, carry):
        pltpu.make_async_remote_copy(
            score_send.at[i],
            score_recv.at[i],
            send_sem.at[2],
            recv_sem.at[2 * GROUPS],
            device_id={"shard": peer(shards - i)},
            device_id_type=MESH,
        ).start()
        return carry

    lax.fori_loop(1, shards, push_scores, 0)
    score_recv[0] = score_send[0]

    placed = [jnp.zeros((docs, LANES), F32) for _ in range(2)]
    for g in range(GROUPS):
        arrived(back, recv_sem.at[GROUPS + g], g)
        for k, part in enumerate(halves_of(back, g)):
            placed[k] = placed[k] + lax.dot_general(
                place[slots_of(g)],
                part,
                TN,
                preferred_element_type=F32,
            )
    for k in range(2):
        enc_ref[:, k * LANES : (k + 1) * LANES] = placed[k].astype(BF16)
    others = score_recv.at[pl.ds(1, shards - 1)]
    pltpu.make_async_copy(others, others, recv_sem.at[2 * GROUPS]).wait()
    message = score_recv[...].reshape(shards, LANES)
    sums = jnp.sum(message, axis=0, keepdims=True)
    pair_total = jnp.maximum(sums[:, 7:8], 1.0)
    found = lax.dot_general(
        message,
        named_f,
        TN,
        precision=lax.Precision.HIGHEST,
        preferred_element_type=F32,
    )
    score_out = jnp.zeros((1, docs), F32)
    grad_out = jnp.zeros((1, docs), F32)
    for r in range(CAP):
        score_out = score_out + jnp.where(rank == r, found[r : r + 1], 0.0)
        grad_out = grad_out + jnp.where(rank == r, found[CAP + r : CAP + r + 1], 0.0)
    small_ref[0:1, :] = score_out
    small_ref[1:2, :] = grad_out / pair_total
    small_ref[2:3, :] = jnp.broadcast_to(sums[:, 6:7] / pair_total, (1, docs))
    small_ref[3:8, :] = jnp.zeros((5, docs), F32)

    for at, ref in enumerate((send, back_send, score_send)):
        first = 1 if ref is score_send else CAP
        sent = ref.at[pl.ds(first, ref.shape[0] - first)]
        pltpu.make_async_copy(sent, sent, send_sem.at[at]).wait()


def body(
    features,
    owners,
    query_local,
    grades,
    query_weight,
    norm_gain,
    qkv_weight,
    out_weight,
    score_weight,
):
    shards = lax.axis_size("shard")
    heads = lax.axis_size("head")
    docs = features.shape[0]
    width, model = out_weight.shape
    slots = CAP * shards
    vmem = pl.BlockSpec(memory_space=pltpu.VMEM)
    hbm = pl.BlockSpec(memory_space=pltpu.HBM)
    dma = pltpu.SemaphoreType.DMA
    def row(x, at):
        return jnp.pad(
            x.reshape(1, -1), ((at, ROWS - 1 - at), (0, model - x.size))
        )

    integers = row(owners, 0) + row(query_local, 1) + row(grades, 2)
    floats = row(score_weight, 3) + row(norm_gain, 4) + row(query_weight, 5)
    small = integers.astype(F32) + floats
    blocks = pltpu.VMEM((slots, 2, LANES), BF16)
    words = pltpu.VMEM((shards, 1, LANES), F32)
    encoded, back_small = pl.pallas_call(
        functools.partial(layer_kernel, shards, heads, query_weight.shape[0]),
        out_shape=(
            jax.ShapeDtypeStruct((docs, width), BF16),
            jax.ShapeDtypeStruct((ROWS, docs), F32),
        ),
        in_specs=[hbm, vmem, hbm, hbm],
        out_specs=(vmem, vmem),
        scratch_shapes=[
            pltpu.VMEM((docs, width), BF16),
            pltpu.VMEM((3, model, width), BF16),
            pltpu.VMEM((heads, width, model), BF16),
            pltpu.VMEM((heads, ROWS, width), F32),
            blocks,
            blocks,
            words,
            words,
            pltpu.VMEM((slots, LANES), F32),
            pltpu.VMEM((heads, slots, width), BF16),
            pltpu.VMEM((slots, 3 * width), BF16),
            pltpu.VMEM((heads, slots, width), BF16),
            pltpu.VMEM((slots * max(SIXTEENTHS) // 16, model), F32),
            blocks,
            blocks,
            words,
            words,
            dma((3,)),
            dma((3,)),
            dma((2 * GROUPS + 1,)),
            dma((2 * GROUPS + 2, heads)),
            dma((2 * GROUPS + 2, heads)),
            dma((heads,)),
            dma((heads,)),
            dma,
            dma,
            dma((heads,)),
            dma((heads,)),
        ],
        compiler_params=pltpu.CompilerParams(
            collective_id=0, has_side_effects=True, vmem_limit_bytes=107 << 19
        ),
    )(
        features,
        small,
        jnp.transpose(qkv_weight, (1, 0, 2)),
        out_weight,
    )
    return encoded, back_small[0], back_small[1], back_small[2, 0]


def solution(mesh):
    placed = (
        P("shard", None),
        P("shard", None),
        P("shard"),
        P("shard"),
        P("shard"),
        P(),
        P(None, None, "head"),
        P("head", None),
        P("head"),
    )
    return jax.shard_map(
        body,
        mesh=mesh,
        in_specs=placed,
        out_specs=(P("shard", "head"), P("shard"), P("shard"), P()),
        check_vma=False,
    )
```

```python
import functools

import jax
import jax.numpy as jnp
from jax import lax
from jax.experimental import pallas as pl
from jax.experimental.pallas import tpu as pltpu
from jax.sharding import PartitionSpec as P

MESH = pl.DeviceIdType.MESH
HEAD_DIM = 64
CAP = 3
ROWS = 8
SIXTEENTHS = (2, 4, 4, 4, 2)
GROUPS = len(SIXTEENTHS)
LANES = 128
eps_norm = 1e-06
F32 = jnp.float32
BF16 = jnp.bfloat16
NT = (((1,), (1,)), ((), ()))
TN = (((0,), (0,)), ((), ()))


def dot(a, b):
    return jnp.dot(a, b, preferred_element_type=F32)


def iota(shape, dim):
    return lax.broadcasted_iota(jnp.int32, shape, dim)


def layer_kernel(
    shards,
    heads,
    query_count,
    feat_hbm,
    inputs_ref,
    wqkv_hbm,
    wout_hbm,
    enc_ref,
    small_ref,
    feat_ref,
    wqkv,
    wout,
    sw_all,
    send,
    recv,
    facts_send,
    facts_recv,
    spread_rows,
    gathered,
    proj,
    context,
    mixed_ref,
    back_send,
    back,
    score_send,
    score_recv,
    local_sem,
    send_sem,
    recv_sem,
    y_send,
    y_recv,
    pair_send,
    pair_recv,
    facts_sent,
    facts_came,
    facts_y_sent,
    facts_y_came,
):
    me = lax.axis_index("shard")
    head = lax.axis_index("head")
    docs = feat_hbm.shape[0]
    width = wout_hbm.shape[0]
    model = wout_hbm.shape[1]
    slots = CAP * shards
    cut = [shards * sum(SIXTEENTHS[:g]) // 16 for g in range(GROUPS + 1)]
    share = shards // heads

    def in_halves(x):
        return jnp.stack([x[:, :LANES], x[:, LANES:]], axis=1).astype(BF16)

    def halves_of(ref, g):
        x = ref[slots_of(g)].astype(F32)
        return [x[:, k, :].astype(BF16) for k in range(2)]

    def slots_of(g):
        return slice(cut[g] * CAP, cut[g + 1] * CAP)

    def peer(i):
        return lax.rem(me + i, shards)

    def head_peer(i):
        return lax.rem(head + i, heads)

    cols = pl.ds(pl.multiple_of(head * width, width), width)
    arguments = (
        (feat_hbm.at[:, cols], feat_ref),
        (wqkv_hbm, wqkv),
        (wout_hbm, wout.at[head]),
    )
    loads = [
        pltpu.make_async_copy(source, target, local_sem.at[k])
        for k, (source, target) in enumerate(arguments)
    ]
    for load in loads:
        load.start()

    barrier = pltpu.get_barrier_semaphore()

    def greet(i, carry):
        pl.semaphore_signal(
            barrier, 1, device_id={"shard": peer(i)}, device_id_type=MESH
        )
        return carry

    lax.fori_loop(1, shards, greet, 0, unroll=True)
    for i in range(1, heads):
        pl.semaphore_signal(
            barrier, 1, device_id={"head": head_peer(i)}, device_id_type=MESH
        )

    owner = jnp.bitwise_and(
        inputs_ref[0:1, :docs].astype(jnp.int32) - me, shards - 1
    )
    query = inputs_ref[1:2, :docs] + 1.0
    grade = inputs_ref[2:3, :docs]
    named = iota((shards, docs), 0) == owner
    named_f = named.astype(F32)
    earlier = (iota((docs, docs), 0) < iota((docs, docs), 1)).astype(F32).astype(BF16)
    before = dot(named_f.astype(BF16), earlier)
    rank_f = jnp.sum(before * named_f, axis=0, keepdims=True)
    rank = rank_f.astype(jnp.int32)
    place = (iota((slots, docs), 0) == owner * CAP + rank).astype(F32).astype(BF16)
    lane = iota((LANES, docs), 0)
    facts = jnp.where(lane == rank, query, 0.0) + jnp.where(
        lane == rank + CAP, grade, 0.0
    )
    loads[0].wait()
    block = dot(place, feat_ref[...])
    send[...] = in_halves(block)
    facts_send[...] = lax.dot_general(
        named_f.astype(BF16), facts.astype(BF16), NT, preferred_element_type=F32
    ).reshape(shards, 1, LANES)
    sw_all[head] = jnp.broadcast_to(inputs_ref[3:4, :width], (ROWS, width))

    def exchange(source, target, step):
        copies = []
        for i in (2, 1, 3):
            copy = pltpu.make_async_remote_copy(
                source,
                target,
                y_send.at[step, i],
                y_recv.at[step, i],
                device_id={"head": head_peer(i)},
                device_id_type=MESH,
            )
            copy.start()
            copies.append(copy)
        return copies

    core = lax.rem(me, 2)
    half_rows = width // 2
    half = pl.ds(pl.multiple_of(core * half_rows, half_rows), half_rows)

    pl.semaphore_wait(barrier, shards - 1 + heads - 1)

    out_copies = exchange(wout_hbm.at[half], wout.at[head, half], 2 * GROUPS)
    sw_copies = exchange(sw_all.at[head], sw_all.at[head], 2 * GROUPS + 1)

    def push_facts(i, carry):
        pltpu.make_async_remote_copy(
            facts_send.at[i],
            facts_recv.at[i],
            facts_sent,
            facts_came,
            device_id={"shard": peer(i)},
            device_id_type=MESH,
        ).start()
        return carry

    for g in range(heads):

        @pl.when(head == g)
        def _(g=g):
            lax.fori_loop(max(1, g * share), (g + 1) * share, push_facts, 0)

    for g in range(GROUPS):

        def push(i, carry, g=g):
            at = pl.ds(i * CAP, CAP)
            pltpu.make_async_remote_copy(
                send.at[at],
                recv.at[at],
                send_sem.at[0],
                recv_sem.at[g],
                device_id={"shard": peer(i)},
                device_id_type=MESH,
            ).start()
            return carry

        lax.fori_loop(max(1, cut[g]), cut[g + 1], push, 0)
    recv[0:CAP] = send[0:CAP]

    def arrived(ref, sem, g):
        low = max(1, cut[g]) * CAP
        some = ref.at[pl.ds(low, cut[g + 1] * CAP - low)]
        pltpu.make_async_copy(some, some, sem).wait()

    def share_facts(g):
        low = max(1, g * share)
        got = facts_recv.at[pl.ds(low, (g + 1) * share - low)]
        all_of = facts_recv.at[pl.ds(g * share, share)]
        mine = head == g

        def to(i):
            return pltpu.make_async_remote_copy(
                all_of,
                all_of,
                facts_y_sent.at[i],
                facts_y_came.at[g],
                device_id={"head": head_peer(i)},
                device_id_type=MESH,
            )

        @pl.when(mine)
        def _():
            if g == 0:
                facts_recv[0] = facts_send[0]
            pltpu.make_async_copy(got, got, facts_came).wait()
            for i in (2, 1, 3):
                to(i).start()

        def finish():
            @pl.when(mine)
            def _():
                for i in (2, 1, 3):
                    to(i).wait_send()
                sent = facts_send.at[pl.ds(low, (g + 1) * share - low)]
                pltpu.make_async_copy(sent, sent, facts_sent).wait()

            @pl.when(jnp.logical_not(mine))
            def _():
                to(1).wait_recv()

        return finish

    for load in loads[1:]:
        load.wait()

    def project(g, copies):
        for copy in copies:
            copy.wait()
        rows = (cut[g + 1] - cut[g]) * CAP
        squares = jnp.zeros((rows, 1), F32)
        total = [jnp.zeros((rows, width), F32) for _ in range(3)]
        for k in range(heads):
            x = gathered[k, slots_of(g), :].astype(F32)
            squares = squares + jnp.sum(x * x, axis=1, keepdims=True)
            scaled = (x * inputs_ref[4:5, k * width : (k + 1) * width]).astype(BF16)
            for j in range(3):
                total[j] = total[j] + dot(scaled, wqkv[j, k * width : (k + 1) * width])
        scale = lax.rsqrt(squares / model + eps_norm)
        for j in range(3):
            proj[slots_of(g), j * width : (j + 1) * width] = (
                total[j] * scale
            ).astype(BF16)

    copies = []
    finish_facts = [share_facts(g) for g in range(heads)]
    for g in range(GROUPS):
        arrived(recv, recv_sem.at[g], g)
        for k, part in enumerate(halves_of(recv, g)):
            gathered[head, slots_of(g), k * LANES : (k + 1) * LANES] = part
        own = gathered.at[head, slots_of(g)]
        copies.append(exchange(own, own, g))
        if g == 1:
            for finish in finish_facts:
                finish()
            lane_col = iota((1, LANES), 1)
            facts = facts_recv[...].reshape(shards, LANES)
            for r in range(CAP):
                spread_rows[pl.ds(r, shards, stride=CAP), :] = jnp.where(
                    lane_col == 0, facts[:, r : r + 1], facts[:, CAP + r : CAP + r + 1]
                )
            diagonal = iota((slots, slots), 0) == iota((slots, slots), 1)

            def to_row(col):
                return jnp.sum(jnp.where(diagonal, col, 0.0), axis=0, keepdims=True)

            query_col, grade_col = spread_rows[:, 0:1], spread_rows[:, 1:2]
            query_row, grade_row = to_row(query_col), to_row(grade_col)
            related = (query_col == query_row) & (query_col > 0.5)
            bias = jnp.where(related | diagonal, 0.0, -jnp.inf)
            above = grade_col - grade_row
            counted = jnp.where(
                related & (above != 0.0), jnp.where(above > 0.0, 1.0, -1.0), 0.0
            )
            weight_col = jnp.zeros((slots, 1), F32)
            for k in range(query_count):
                weight_col = weight_col + jnp.where(
                    query_col == float(k + 1), inputs_ref[5:6, k : k + 1], 0.0
                )
        if g >= 2:
            project(g - 2, copies[g - 2])
    project(GROUPS - 2, copies[GROUPS - 2])

    for copy in out_copies + sw_copies:
        copy.wait()
    pair_copies = []
    for i in range(1, heads):
        piece = wout.at[lax.rem(head + heads - i, heads), half]
        copy = pltpu.make_async_remote_copy(
            piece,
            piece,
            pair_send.at[i],
            pair_recv.at[i],
            device_id={"shard": me + 1 - 2 * core},
            device_id_type=MESH,
        )
        copy.start()
        pair_copies.append(copy)
    project(GROUPS - 1, copies[GROUPS - 1])

    keys_t = proj[:, width : 2 * width].T
    copies = []
    for g in range(GROUPS):
        for pair in range(width // LANES):
            at = pair * LANES
            q2 = proj[slots_of(g), at : at + LANES] * jnp.asarray(HEAD_DIM**-0.5, BF16)
            k2 = keys_t[at : at + LANES, :]
            v2 = proj[:, 2 * width + at : 2 * width + at + LANES]
            halves = [
                jnp.where((lane_col // HEAD_DIM) == sub, q2, jnp.zeros_like(q2))
                for sub in range(LANES // HEAD_DIM)
            ]
            scores = dot(jnp.concatenate(halves, axis=0), k2) + jnp.concatenate(
                [bias[slots_of(g), :]] * 2, axis=0
            )
            expo = jnp.exp(scores - jnp.max(scores, axis=1, keepdims=True))
            whole = 1.0 / jnp.sum(expo, axis=1, keepdims=True)
            out = dot(expo.astype(BF16), v2) * whole
            rows = (cut[g + 1] - cut[g]) * CAP
            both_heads = jnp.where(lane_col < HEAD_DIM, out[:rows], out[rows:])
            context[head, slots_of(g), at : at + LANES] = both_heads.astype(BF16)
        own = context.at[head, slots_of(g)]
        copies.append(exchange(own, own, GROUPS + g))
    for copy in pair_copies:
        copy.wait()

    score_cols = []
    for g in range(GROUPS):
        for copy in copies[g]:
            copy.wait()
        attended = dot(context[0, slots_of(g), :], wout[0])
        for k in range(1, heads):
            attended = attended + dot(context[k, slots_of(g), :], wout[k])
        rows = (cut[g + 1] - cut[g]) * CAP
        squares = jnp.zeros((rows, 1), F32)
        weighted = jnp.zeros((rows, 1), F32)
        for k in range(heads):
            mixed = (
                gathered[k, slots_of(g), :].astype(F32)
                + attended[:, k * width : (k + 1) * width]
            )
            mixed_ref[0:rows, k * width : (k + 1) * width] = mixed
            squares = squares + jnp.sum(mixed * mixed, axis=1, keepdims=True)
            weighted = weighted + jnp.sum(
                mixed * sw_all[k, 0:1, :], axis=1, keepdims=True
            )
        score_cols.append(weighted * lax.rsqrt(squares / model + eps_norm))
        back_send[slots_of(g)] = in_halves(mixed_ref[0:rows, cols])

        def push_back(i, carry, g=g):
            at = pl.ds(i * CAP, CAP)
            pltpu.make_async_remote_copy(
                back_send.at[at],
                back.at[at],
                send_sem.at[1],
                recv_sem.at[GROUPS + g],
                device_id={"shard": peer(shards - i)},
                device_id_type=MESH,
            ).start()
            return carry

        if g < GROUPS - 1:
            lax.fori_loop(max(1, cut[g]), cut[g + 1], push_back, 0)
    back[0:CAP] = back_send[0:CAP]

    score_col = jnp.concatenate(score_cols, axis=0)
    spread = counted * (to_row(score_col) - score_col)
    small = jnp.exp(-jnp.abs(spread))
    softplus = jnp.maximum(spread, 0.0) + jnp.log1p(small)
    sigmoid = jnp.where(spread >= 0.0, 1.0, small) / (1.0 + small)
    both = jnp.abs(counted)
    pull_col = -weight_col * jnp.sum(counted * sigmoid, axis=1, keepdims=True)
    pair_col = weight_col * jnp.sum(both * softplus, axis=1, keepdims=True)
    pair_sum = 0.5 * jnp.sum(pair_col, axis=0, keepdims=True)
    pair_count = 0.5 * jnp.sum(
        jnp.sum(both, axis=1, keepdims=True), axis=0, keepdims=True
    )

    spread_rows[...] = jnp.where(lane_col == 0, score_col, pull_col)
    by_rank = [spread_rows[pl.ds(r, shards, stride=CAP), :] for r in range(CAP)]
    words = [x[:, 0:1] for x in by_rank] + [x[:, 1:2] for x in by_rank]
    words += [pair_sum, pair_count]
    message = jnp.zeros((shards, LANES), F32)
    for k, word in enumerate(words):
        message = jnp.where(lane_col == k, word, message)
    score_send[...] = message.reshape(shards, 1, LANES)

    def push_scores(i, carry):
        pltpu.make_async_remote_copy(
            score_send.at[i],
            score_recv.at[i],
            send_sem.at[2],
            recv_sem.at[2 * GROUPS],
            device_id={"shard": peer(shards - i)},
            device_id_type=MESH,
        ).start()
        return carry

    lax.fori_loop(1, shards, push_scores, 0)
    lax.fori_loop(cut[GROUPS - 1], shards, push_back, 0)
    score_recv[0] = score_send[0]

    placed = [jnp.zeros((docs, LANES), F32) for _ in range(2)]
    for g in range(GROUPS):
        arrived(back, recv_sem.at[GROUPS + g], g)
        for k, part in enumerate(halves_of(back, g)):
            placed[k] = placed[k] + lax.dot_general(
                place[slots_of(g)],
                part,
                TN,
                preferred_element_type=F32,
            )
    for k in range(2):
        enc_ref[:, k * LANES : (k + 1) * LANES] = placed[k].astype(BF16)
    others = score_recv.at[pl.ds(1, shards - 1)]
    pltpu.make_async_copy(others, others, recv_sem.at[2 * GROUPS]).wait()
    message = score_recv[...].reshape(shards, LANES)
    sums = jnp.sum(message, axis=0, keepdims=True)
    pair_total = jnp.maximum(sums[:, 7:8], 1.0)
    found = lax.dot_general(
        message,
        named_f,
        TN,
        precision=lax.Precision.HIGHEST,
        preferred_element_type=F32,
    )
    score_out = jnp.zeros((1, docs), F32)
    grad_out = jnp.zeros((1, docs), F32)
    for r in range(CAP):
        score_out = score_out + jnp.where(rank == r, found[r : r + 1], 0.0)
        grad_out = grad_out + jnp.where(rank == r, found[CAP + r : CAP + r + 1], 0.0)
    small_ref[0:1, :] = score_out
    small_ref[1:2, :] = grad_out / pair_total
    small_ref[2:3, :] = jnp.broadcast_to(sums[:, 6:7] / pair_total, (1, docs))
    small_ref[3:8, :] = jnp.zeros((5, docs), F32)

    for at, ref in enumerate((send, back_send, score_send)):
        first = 1 if ref is score_send else CAP
        sent = ref.at[pl.ds(first, ref.shape[0] - first)]
        pltpu.make_async_copy(sent, sent, send_sem.at[at]).wait()


def body(
    features,
    owners,
    query_local,
    grades,
    query_weight,
    norm_gain,
    qkv_weight,
    out_weight,
    score_weight,
):
    shards = lax.axis_size("shard")
    heads = lax.axis_size("head")
    docs = features.shape[0]
    width, model = out_weight.shape
    slots = CAP * shards
    vmem = pl.BlockSpec(memory_space=pltpu.VMEM)
    hbm = pl.BlockSpec(memory_space=pltpu.HBM)
    dma = pltpu.SemaphoreType.DMA
    def row(x, at):
        return jnp.pad(
            x.reshape(1, -1), ((at, ROWS - 1 - at), (0, model - x.size))
        )

    integers = row(owners, 0) + row(query_local, 1) + row(grades, 2)
    floats = row(score_weight, 3) + row(norm_gain, 4) + row(query_weight, 5)
    small = integers.astype(F32) + floats
    blocks = pltpu.VMEM((slots, 2, LANES), BF16)
    words = pltpu.VMEM((shards, 1, LANES), F32)
    encoded, back_small = pl.pallas_call(
        functools.partial(layer_kernel, shards, heads, query_weight.shape[0]),
        out_shape=(
            jax.ShapeDtypeStruct((docs, width), BF16),
            jax.ShapeDtypeStruct((ROWS, docs), F32),
        ),
        in_specs=[hbm, vmem, hbm, hbm],
        out_specs=(vmem, vmem),
        scratch_shapes=[
            pltpu.VMEM((docs, width), BF16),
            pltpu.VMEM((3, model, width), BF16),
            pltpu.VMEM((heads, width, model), BF16),
            pltpu.VMEM((heads, ROWS, width), F32),
            blocks,
            blocks,
            words,
            words,
            pltpu.VMEM((slots, LANES), F32),
            pltpu.VMEM((heads, slots, width), BF16),
            pltpu.VMEM((slots, 3 * width), BF16),
            pltpu.VMEM((heads, slots, width), BF16),
            pltpu.VMEM((slots * max(SIXTEENTHS) // 16, model), F32),
            blocks,
            blocks,
            words,
            words,
            dma((3,)),
            dma((3,)),
            dma((2 * GROUPS + 1,)),
            dma((2 * GROUPS + 2, heads)),
            dma((2 * GROUPS + 2, heads)),
            dma((heads,)),
            dma((heads,)),
            dma,
            dma,
            dma((heads,)),
            dma((heads,)),
        ],
        compiler_params=pltpu.CompilerParams(
            collective_id=0, has_side_effects=True, vmem_limit_bytes=107 << 19
        ),
    )(
        features,
        small,
        jnp.transpose(qkv_weight, (1, 0, 2)),
        out_weight,
    )
    return encoded, back_small[0], back_small[1], back_small[2, 0]


def solution(mesh):
    placed = (
        P("shard", None),
        P("shard", None),
        P("shard"),
        P("shard"),
        P("shard"),
        P(),
        P(None, None, "head"),
        P("head", None),
        P("head"),
    )
    return jax.shard_map(
        body,
        mesh=mesh,
        in_specs=placed,
        out_specs=(P("shard", "head"), P("shard"), P("shard"), P()),
        check_vma=False,
    )
```
